32 devices in a mesh: dp: 8 (over z, y), mp: 4 (over x, core).
Axes of the slice: x: 2, y: 2, z: 4, core: 2. Of those that a mesh axis runs over, the one named last changes fastest.
Arguments:
- queries: bfloat16 [4096, 2048], P('dp', 'mp'), may hold values from -96 to 96
- out_grad: bfloat16 [4096, 2048], P('dp', 'mp'), may hold values from -0.75 to 0.75
- owner: int32 [64, 2], P('dp'), may hold values from 0 to 7, all different within a row; in each aligned block of 8 rows (0 to 7, 8 to 15, ...) at most 2 rows name the same one
- store_row: int32 [64, 2], P('dp'), may hold values from 0 to 1
- store: bfloat16 [16, 128, 4096], P('dp', None, 'mp'), may hold values from -80 to 80
- norm_gain: bfloat16 [4096], P('mp'), may hold values from 0.5 to 2
- w_key: bfloat16 [4096, 2048], P(None, 'mp'), may hold values from -0.09375 to 0.09375
- w_value: bfloat16 [4096, 2048], P(None, 'mp'), may hold values from -0.09375 to 0.09375
Outputs:
- attended: bfloat16 [4096, 2048], P('dp', 'mp')
- query_grad: bfloat16 [4096, 2048], P('dp', 'mp')
- key_weight_grad: float32 [4096, 2048], P('dp', 'mp')
- value_weight_grad: float32 [4096, 2048], P('dp', 'mp')
The draws below stay inside these ranges and needn't reach their ends.
Inputs may be any that keep to these rules, and one draw needn't show every extreme that they name: Within the 8 spans of one index of dp no owner is named more than 2 times, and in some such block one owner is named exactly 2 times; the 2 neighbours of a span have different owners.
All inputs are finite; a program needn't handle non-finite values.
Results may differ from the reference program's by a relative error of at most 0.03.
The reference program's roundings to bfloat16 on the way count: a program that leaves them out, or rounds other values in their place, can miss the bound.
Values may be sent and summed in bfloat16 or wider, within the bound.
No kernel may reach another device: no remote copies, remote signals or barrier semaphores. Data moves between devices by JAX's collectives and lax.ppermute only.
A program may use at most 128 MiB of HBM per device.

```python
import math
import jax
import jax.numpy as jnp
import numpy as np
from jax import lax

D = 4096
HEADS = 16
HEAD = 128
SPAN = 64
NLEN = 128
NBR = 2
CH_DEV = 8
STORE_DEV = 2
CAP = 2
SPANS = 64
TOKENS = 4096
STORES = 16
N_DP = 8


def draw_queries(key, part):
    key = jax.random.fold_in(key, 11)
    subkeys = jax.random.split(key, 1)
    shape = (TOKENS, HEADS * HEAD)
    base = jax.random.normal(subkeys[0], shape, jnp.float32) * 2.0
    return jnp.clip(base, -96.0, 96.0).astype(jnp.bfloat16)


def draw_store(key, part):
    key = jax.random.fold_in(key, 23)
    subkeys = jax.random.split(key, 2)
    shape = (STORES, NLEN, D)
    row_scale = jnp.exp(jax.random.uniform(subkeys[1], (STORES, NLEN, 1), jnp.float32, 0.0, 2.302585))
    base = jax.random.normal(subkeys[0], shape, jnp.float32)
    return jnp.clip(base * row_scale, -80.0, 80.0).astype(jnp.bfloat16)


def place_ends(drawn, rng, least, top_value):
    spot = [jax.random.randint(jax.random.fold_in(rng, axis), (), 0, length) for axis, length in enumerate(drawn.shape)]
    widest = drawn.shape.index(max(drawn.shape))
    neighbour = spot[:widest] + [(spot[widest] + 1) % drawn.shape[widest]] + spot[widest + 1:]
    return drawn.at[tuple(spot)].set(least).at[tuple(neighbour)].set(top_value)


def block_levels(stream_key, shape, pieces, least, high):
    factor_of, own = 1.0, jax.random.fold_in(stream_key, 6)
    for dim, blocks in pieces:
        steps = jnp.exp(jax.random.uniform(jax.random.fold_in(own, dim), (blocks,), jnp.float32, least / len(pieces), high / len(pieces)))
        factor_of = factor_of * jnp.repeat(steps, shape[dim] // blocks).reshape([-1 if axis == dim else 1 for axis in range(len(shape))])
    return factor_of


def deal_out(stream_key, own, number, rows, amount, top, limit, lean):
    ranking = jax.random.permutation(stream_key, amount)
    crowded, common = portions_of(amount, rows * top, limit, lean, True), portions_of(amount, rows * top, limit, lean, False)
    places = jnp.arange(amount)

    def named(tallies, rotation):
        used = int((tallies > 0).sum())
        fixed = max(1, used // 4)
        shifted = fixed + (places - fixed + rotation * (used - fixed)) % max(1, amount - fixed)
        return jnp.zeros((amount,), jnp.int32).at[ranking[jnp.where(places < fixed, places, shifted)]].set(jnp.asarray(tallies, jnp.int32))

    tallies = jnp.where(number % 4 == 0, named(crowded, number // 4), named(common, number - number // 4 - 1))
    mixed = jax.random.permutation(jax.random.fold_in(own, 3), amount)
    donor, taker = mixed[0:amount // 2 * 2:2], mixed[1:amount // 2 * 2:2]
    slack = jnp.minimum(tallies[donor] - 1, limit - tallies[taker]) // 2
    slack = jnp.where((donor == ranking[0]) | (taker == ranking[0]) | (tallies[taker] == 0), 0, jnp.maximum(slack, 0))
    shifted = jax.random.randint(jax.random.fold_in(own, 4), (amount // 2,), 0, 1 << 20) % (slack + 1)
    tallies = tallies.at[donor].add(-shifted).at[taker].add(shifted)
    items = jnp.searchsorted(jnp.cumsum(tallies), jnp.arange(rows * top), side="right").astype(jnp.int32)
    grid = items.reshape(top, rows).T
    grid = grid[jax.random.permutation(jax.random.fold_in(own, 1), rows)]
    rotation = jax.random.randint(jax.random.fold_in(own, 2), (rows, 1), 0, top)
    return jnp.take_along_axis(grid, (jnp.arange(top)[None, :] + rotation) % top, axis=1)


def portions_of(number_of, total, bound, skew, full):
    weights = [(1 << 20) // math.isqrt(grade ** skew) + 1 for grade in range(1, number_of + 1)]
    largest = bound if full else min(bound, max(-(-total // number_of), total * weights[0] // sum(weights)))
    least = 1 if total - largest >= number_of - 1 else 0
    given, spare = [largest] + [least] * (number_of - 1), total - largest - least * (number_of - 1)
    while spare > 0:
        movable = [i for i in range(1, number_of) if given[i] < largest] or [i for i in range(1, number_of) if given[i] < bound]
        whole, remaining = sum([weights[i] for i in movable]), spare
        for i in movable:
            addition = min(bound - given[i], max(1, remaining * weights[i] // whole), spare)
            given[i] = given[i] + addition
            spare = spare - addition
    return np.array(given)


def bell_draw(own_key, dims, scale, reach, cuts=(), dtype=jnp.bfloat16):
    drawn = scale * jax.random.normal(own_key, dims, jnp.float32)
    if cuts:
        drawn = drawn * block_levels(own_key, dims, cuts, -0.22, 0.18)
    return jnp.clip(drawn, -reach, reach).astype(dtype)


def setup_inputs(seed: int = 0) -> dict:
    arg_keys = jax.random.split(jax.random.key(seed), 9)
    queries = draw_queries(jax.random.fold_in(arg_keys[8], 71), 0)
    out_grad = bell_draw(arg_keys[1], (TOKENS, HEADS * HEAD), 0.125, 0.75, ((0, 8), (1, 4)))
    owner_keys = jax.random.split(jax.random.fold_in(arg_keys[2], 1), SPANS // CH_DEV)
    owner_turns = jax.random.permutation(jax.random.fold_in(arg_keys[2], 3), SPANS // CH_DEV)
    owner = jax.vmap(lambda own, number: deal_out(jax.random.fold_in(arg_keys[2], 2), own, number, CH_DEV, N_DP, NBR, CAP, 2))(owner_keys, owner_turns).reshape((SPANS, NBR))
    store_row = place_ends(jax.random.randint(arg_keys[3], (SPANS, NBR), 0, STORE_DEV), jax.random.fold_in(arg_keys[3], 1), 0, STORE_DEV - 1).astype(jnp.int32)
    store = draw_store(jax.random.fold_in(arg_keys[8], 71), 0)
    norm_gain = jnp.clip(jnp.exp(math.log(2.0) - 1.3862944 * jax.random.uniform(arg_keys[5], (D,), jnp.float32) ** block_levels(arg_keys[5], (D,), ((0, 4),), -0.2, 0.2)), 0.5, 2.0).astype(jnp.bfloat16)
    w_key = bell_draw(arg_keys[6], (D, HEADS * HEAD), D ** -0.5, 0.09375, ((1, 4),))
    w_value = bell_draw(arg_keys[7], (D, HEADS * HEAD), D ** -0.5, 0.09375, ((1, 4),))
    return dict(queries=queries, out_grad=out_grad, owner=owner, store_row=store_row, store=store, norm_gain=norm_gain, w_key=w_key, w_value=w_value)


epsilon = 1e-06

def reference(queries, out_grad, owner, store_row, store, norm_gain, w_key, w_value):
    model_width = HEADS * HEAD
    floats = store.astype(jnp.float32)
    scale_rows = lax.rsqrt(lax.optimization_barrier(jnp.mean(floats * floats, axis=-1, keepdims=True)) + epsilon)
    normed = (floats * scale_rows * norm_gain.astype(jnp.float32)).astype(jnp.bfloat16).reshape(STORES * NLEN, D)
    key_rows = jnp.dot(normed, w_key, preferred_element_type=jnp.float32).astype(jnp.bfloat16).reshape(STORES, NLEN, model_width)
    value_rows = jnp.dot(normed, w_value, preferred_element_type=jnp.float32).astype(jnp.bfloat16).reshape(STORES, NLEN, model_width)
    inverse_root = 1.0 / math.sqrt(HEAD)
    references = CH_DEV * NBR
    earlier = jnp.tril(jnp.ones((references, references), jnp.float32), -1)
    query_blocks = queries.reshape(N_DP, CH_DEV, SPAN, HEADS, HEAD)
    grad_blocks = out_grad.reshape(N_DP, CH_DEV, SPAN, HEADS, HEAD)
    id_blocks = (owner.astype(jnp.int32) * STORE_DEV + store_row.astype(jnp.int32)).astype(jnp.int32).reshape(N_DP, references)

    def block_step(state_pair, block_args):
        acc_key, acc_value = state_pair
        query_blk, grad_blk, global_id = block_args
        query_f = query_blk.astype(jnp.float32)
        grad_f = grad_blk.astype(jnp.float32)
        key_ctx = jnp.take(key_rows, global_id, axis=0).reshape(CH_DEV, NBR * NLEN, HEADS, HEAD).astype(jnp.float32)
        value_ctx = jnp.take(value_rows, global_id, axis=0).reshape(CH_DEV, NBR * NLEN, HEADS, HEAD).astype(jnp.float32)
        scores = jnp.einsum('cqhd,ckhd->chqk', query_f, key_ctx) * inverse_root
        probs = jax.nn.softmax(scores, axis=-1)
        probs_low = lax.optimization_barrier(probs.astype(jnp.bfloat16)).astype(jnp.float32)
        attended_blk = jnp.einsum('chqk,ckhd->cqhd', probs_low, value_ctx).astype(jnp.bfloat16)
        prob_grad = jnp.einsum('cqhd,ckhd->chqk', grad_f, value_ctx)
        row_delta = lax.optimization_barrier(jnp.sum(probs * prob_grad, axis=-1, keepdims=True))
        score_grad = lax.optimization_barrier((probs * (prob_grad - row_delta)).astype(jnp.bfloat16)).astype(jnp.float32)
        query_grad_blk = (jnp.einsum('chqk,ckhd->cqhd', score_grad, key_ctx) * inverse_root).astype(jnp.bfloat16)
        key_grad = jnp.einsum('chqk,cqhd->ckhd', score_grad, query_f) * inverse_root
        value_grad = jnp.einsum('chqk,cqhd->ckhd', probs_low, grad_f)
        same_id = (global_id[:, None] == global_id[None, :]).astype(jnp.float32)
        first_use = lax.optimization_barrier(jnp.sum(same_id * earlier, axis=1)) == 0.0
        summed_key = jnp.einsum('ij,jtc->itc', same_id, key_grad.reshape(references, NLEN, model_width), precision=lax.Precision.HIGHEST)
        summed_value = jnp.einsum('ij,jtc->itc', same_id, value_grad.reshape(references, NLEN, model_width), precision=lax.Precision.HIGHEST)
        sent_key = lax.optimization_barrier(jnp.where(first_use[:, None, None], summed_key, 0.0).astype(jnp.bfloat16)).astype(jnp.float32)
        sent_value = lax.optimization_barrier(jnp.where(first_use[:, None, None], summed_value, 0.0).astype(jnp.bfloat16)).astype(jnp.float32)
        acc_key = acc_key.at[global_id].add(sent_key)
        acc_value = acc_value.at[global_id].add(sent_value)
        return ((acc_key, acc_value), (attended_blk, query_grad_blk))
    start_grads = (jnp.zeros((STORES, NLEN, model_width), jnp.float32), jnp.zeros((STORES, NLEN, model_width), jnp.float32))
    (sum_key, sum_value), (attended, query_grad) = lax.scan(block_step, start_grads, (query_blocks, grad_blocks, id_blocks))
    row_key = sum_key.astype(jnp.bfloat16).reshape(N_DP, STORE_DEV * NLEN, model_width)
    row_value = sum_value.astype(jnp.bfloat16).reshape(N_DP, STORE_DEV * NLEN, model_width)
    normed_blocks = normed.reshape(N_DP, STORE_DEV * NLEN, D)

    def weight_step(state_pair, block_args):
        normed_blk, key_blk, value_blk = block_args
        key_term = jnp.dot(normed_blk.T, key_blk, preferred_element_type=jnp.float32)
        value_term = jnp.dot(normed_blk.T, value_blk, preferred_element_type=jnp.float32)
        key_term = lax.optimization_barrier(key_term.astype(jnp.bfloat16)).astype(jnp.float32)
        value_term = lax.optimization_barrier(value_term.astype(jnp.bfloat16)).astype(jnp.float32)
        return ((state_pair[0] + key_term, state_pair[1] + value_term), None)
    start_weights = (jnp.zeros((D, model_width), jnp.float32), jnp.zeros((D, model_width), jnp.float32))
    (key_weight_grad, value_weight_grad), unused = lax.scan(weight_step, start_weights, (normed_blocks, row_key, row_value))
    attended = attended.reshape(TOKENS, model_width)
    query_grad = query_grad.reshape(TOKENS, model_width)
    return (attended, query_grad, key_weight_grad, value_weight_grad)
```

```python
import functools
import math

import jax
import jax.numpy as jnp
from jax import lax
from jax.experimental import pallas as pl
from jax.experimental.pallas import tpu as pltpu
from jax.sharding import PartitionSpec as P

HEAD = 128
TILE = 16


epsilon = 1e-06

def params(mebibytes):
    return pltpu.CompilerParams(vmem_limit_bytes=mebibytes * 1024 * 1024)


VMEM = pl.BlockSpec(memory_space=pltpu.VMEM)
SMEM = pl.BlockSpec(memory_space=pltpu.SMEM)
ANY = pl.BlockSpec(memory_space=pl.ANY)
HBM = pl.BlockSpec(memory_space=pltpu.HBM)


def column(head):
    return pl.ds(pl.multiple_of(head * HEAD, HEAD), HEAD)


def pack_kernel(chain, slots, place, owner, store_row, queries, out_grad, store, gain, *refs):
    packed, (bundle, sems, sem) = refs[:chain], refs[chain:]
    tokens, rows = queries.shape[0], store.shape[0]
    named, spans = owner.shape
    copies = [pltpu.make_async_copy(store, bundle.at[pl.ds(0, rows), :], sem)] + [
        pltpu.make_async_copy(
            source.at[:, column(place[0] ^ r)],
            packed[r].at[pl.ds(side * tokens, tokens), :],
            sems.at[r, side],
        )
        for r in range(chain)
        for side, source in enumerate((queries, out_grad))
    ]
    for copy in copies:
        copy.start()
    bundle[pl.ds(rows, TILE), :] = jnp.broadcast_to(gain[...].reshape(1, store.shape[1]), (TILE, store.shape[1]))
    line = lax.broadcasted_iota(jnp.int32, (spans * named, HEAD), 0)
    block = jnp.zeros((spans * named, HEAD), jnp.int32)
    for i in range(spans * named):
        spot = (i % named, i // named)
        block = jnp.where(line == i, owner[spot] * slots + store_row[spot], block)
    block = block.astype(jnp.float32).astype(jnp.bfloat16)
    for r in range(chain):
        packed[r][pl.ds(2 * tokens, spans * named), :] = block
    for copy in copies:
        copy.wait()


def unpack_kernel(chain, place, *refs):
    parts, (attended, query_grad) = refs[:chain - 1], refs[chain - 1:]
    for r, part in enumerate(parts):
        attended[:, column(place[0] ^ r)] = part[0]
        query_grad[:, column(place[0] ^ r)] = part[1]


MASKS = (0, 3, 1, 2)


def mask(m):
    return sum(jnp.where(m == i, x, 0) for i, x in enumerate(MASKS))


def project_kernel(chain, features, place, w_key, w_value, *refs):
    shards = len(refs) - chain - 4
    states, refs = refs[:shards], refs[shards:]
    encoded, (normed_own, normed, weights, sems) = refs[:chain], refs[chain:]
    copies = [
        pltpu.make_async_copy(
            source.at[:, column(place[0] ^ r)],
            weights.at[r, :, pl.ds(side * HEAD, HEAD)],
            sems.at[r, side],
        )
        for r in range(chain)
        for side, source in enumerate((w_key, w_value))
    ]
    for copy in copies:
        copy.start()
    m = place[2]
    rows, width = normed_own.shape
    gain = [x[pl.ds(rows, TILE), :].astype(jnp.float32) for x in states]

    def norm_tile(i, carry):
        part = pl.ds(pl.multiple_of(i * TILE, TILE), TILE)
        square = jnp.zeros((TILE, 1), jnp.float32)
        for x in states:
            floats = x[part, :].astype(jnp.float32)
            square += jnp.sum(floats * floats, axis=-1, keepdims=True)
        scale = lax.rsqrt(square / features + epsilon)
        for q, x in enumerate(states):
            low = (x[part, :].astype(jnp.float32) * scale * gain[q]).astype(jnp.bfloat16)
            normed[part, pl.ds(pl.multiple_of((m ^ q) * width, width), width)] = low
        return carry

    lax.fori_loop(0, rows // TILE, norm_tile, 0, unroll=2)
    block = place[0] ^ mask(m)
    normed_own[...] = normed[:, pl.ds(pl.multiple_of(block * width, width), width)]
    for r in range(chain):
        copies[2 * r].wait()
        copies[2 * r + 1].wait()
        encoded[r][...] = jnp.dot(
            normed[...], weights[r], preferred_element_type=jnp.float32
        ).astype(jnp.bfloat16)


def dot_t(left, right):
    return lax.dot_general(
        left, right, (((1,), (1,)), ((), ())), preferred_element_type=jnp.float32
    )


def dot_0(left, right):
    return lax.dot_general(
        left, right, (((0,), (0,)), ((), ())), preferred_element_type=jnp.float32
    )


def attend_kernel(chain, spans, slots, length, place, *refs):
    asked, refs = refs[:chain], refs[chain:]
    near, far, refs = refs[:chain], refs[chain:2 * chain], refs[2 * chain:]
    given, again, refs = refs[:chain], refs[chain], refs[chain + 1:]
    kept, sent, context, grads, scores, prob_grads, lows, score_grads, lines, ids, sem = refs
    a, y = place[0], place[1]
    tokens = given[0].shape[1]
    span_len = tokens // spans
    pairs = spans // 2
    width = 2 * span_len
    named = 2 * spans
    inverse_root = 1.0 / math.sqrt(HEAD)
    for r in range(chain):
        lines[r] = asked[r][pl.ds(2 * tokens, named), :].astype(jnp.float32).astype(jnp.int32)
    copy = pltpu.make_async_copy(lines, ids, sem)
    copy.start()
    for r in range(chain):
        first = (a ^ r) * 2 * slots
        for s in range(slots):
            context[first + y * slots + s] = near[r][pl.ds(s * length, length), :]
            context[first + (1 - y) * slots + s] = far[r][pl.ds(s * length, length), :]
    grads[...] = jnp.zeros_like(grads)
    copy.wait()

    def fetch(r, c):
        rows = [[ids[r, 4 * c + 2 * h + n, 0] for n in range(2)] for h in range(2)]
        key = [jnp.concatenate([context[i, :, :HEAD] for i in row], axis=0) for row in rows]
        value = [jnp.concatenate([context[i, :, HEAD:] for i in row], axis=0) for row in rows]
        query = asked[r][pl.ds(pl.multiple_of(c * width, width), width), :]
        grad = asked[r][pl.ds(pl.multiple_of(tokens + c * width, width), width), :]
        return rows, key, value, query, grad

    def products(c, carry):
        first = lax.broadcasted_iota(jnp.int32, (2 * length, width), 1) < span_len
        for r in range(chain):
            rows, key, value, query, grad = fetch(r, c)
            scores[r, c] = jnp.where(first, dot_t(key[0], query), dot_t(key[1], query))
            prob_grads[r, c] = jnp.where(first, dot_t(value[0], grad), dot_t(value[1], grad))
        return carry

    lax.fori_loop(0, pairs, products, 0)

    def soften(c, carry):
        for r in range(chain):
            score = scores[r, c] * inverse_root
            powers = jnp.exp(score - jnp.max(score, axis=0, keepdims=True))
            probs = powers * (1.0 / jnp.sum(powers, axis=0, keepdims=True))
            lows[r, c] = probs.astype(jnp.bfloat16)
            prob_grad = prob_grads[r, c]
            delta = jnp.sum(probs * prob_grad, axis=0, keepdims=True)
            score_grads[r, c] = (probs * (prob_grad - delta)).astype(jnp.bfloat16)
        return carry

    lax.fori_loop(0, pairs, soften, 0)

    def results(c, carry):
        upper = lax.broadcasted_iota(jnp.int32, (width, HEAD), 0) < span_len
        both = pl.ds(pl.multiple_of(c * width, width), width)
        for r in range(chain):
            rows, key, value, query, grad = fetch(r, c)
            low, score_grad = lows[r, c], score_grads[r, c]
            for h in range(2):
                mine = upper if h == 0 else jnp.logical_not(upper)
                key_part = jnp.dot(
                    score_grad,
                    jnp.where(mine, query, jnp.zeros_like(query)),
                    preferred_element_type=jnp.float32,
                )
                value_part = jnp.dot(
                    low,
                    jnp.where(mine, grad, jnp.zeros_like(grad)),
                    preferred_element_type=jnp.float32,
                )
                for n in range(2):
                    part = slice(n * length, (n + 1) * length)
                    grads[rows[h][n], :, :HEAD] += key_part[part]
                    grads[rows[h][n], :, HEAD:] += value_part[part]
            attended = jnp.where(upper, dot_0(low, value[0]), dot_0(low, value[1]))
            query_grad = jnp.where(upper, dot_0(score_grad, key[0]), dot_0(score_grad, key[1]))
            given[r][0, both, :] = attended.astype(jnp.bfloat16)
            given[r][1, both, :] = (query_grad * inverse_root).astype(jnp.bfloat16)
        return carry

    lax.fori_loop(0, pairs, results, 0)
    again[...] = given[chain - 1][...]
    for member in range(chain):
        for s in range(slots):
            part = pl.ds(s * length, length)
            own = member * 2 * slots + y * slots + s
            other = member * 2 * slots + (1 - y) * slots + s
            kept[member, part, :HEAD] = grads[own, :, :HEAD] * inverse_root
            kept[member, part, HEAD:] = grads[own, :, HEAD:]
            sent[member, part, :HEAD] = (grads[other, :, :HEAD] * inverse_root).astype(jnp.bfloat16)
            sent[member, part, HEAD:] = grads[other, :, HEAD:].astype(jnp.bfloat16)


def turn_kernel(*refs):
    count = len(refs) // 2
    for share, result in zip(refs[:count], refs[count:]):
        half = result.shape[1]
        for side in range(2):
            result[side] = share[:, side * half:(side + 1) * half].T


def inner(place):
    return (place[0] == 1) | (place[0] == 2)


def weigh_kernel(chain, wants, place, *refs):
    shares, refs = refs[:chain], refs[chain + 1:]
    sources, targets = refs[:-len(wants)], refs[-len(wants):]

    def multiply(row_grad):
        for want, target in zip(wants, targets):
            half = place[1] if want else 1 - place[1]
            total = sum(
                jnp.dot(
                    shares[q][half],
                    row_grad[place[0] ^ mask(place[2] ^ q)],
                    preferred_element_type=jnp.float32,
                )
                for q in range(chain)
            )
            target[...] = total.astype(target.dtype)

    if len(sources) == 1:
        multiply(sources[0])
    else:
        pl.when(inner(place))(lambda: multiply(sources[0]))
        pl.when(jnp.logical_not(inner(place)))(lambda: multiply(sources[1]))


def collect_kernel(chain, place, *refs):
    count = chain - 1
    kept, received, (key_grad, value_grad) = refs[:count], refs[count:2 * count], refs[2 * count:]
    a = place[0]
    turned = inner(place).astype(jnp.int32)
    for r, head in enumerate((a, a ^ 1, a ^ (2 + turned))):
        total = kept[r][...] + received[r][...].astype(jnp.float32)
        key_grad[:, column(head)] = total[:, :HEAD]
        value_grad[:, column(head)] = total[:, HEAD:]


def finish_kernel(chain, place, kept, received, near, far, *refs):
    targets, (total, sems) = refs[4:8], refs[8:]
    apart = inner(place)

    def write(part):
        copies = [
            pltpu.make_async_copy(
                part.at[side], targets[side].at[:, column(place[0] ^ (chain - 1))], sems.at[side]
            )
            for side in range(2)
        ]
        for copy in copies:
            copy.start()
        total[...] = kept[...] + received[...].astype(jnp.float32)
        copies += [
            pltpu.make_async_copy(
                total.at[:, pl.ds(side * HEAD, HEAD)],
                targets[2 + side].at[:, column(place[0] ^ (3 - apart.astype(jnp.int32)))],
                sems.at[2 + side],
            )
            for side in range(2)
        ]
        for copy in copies[2:]:
            copy.start()
        for copy in copies:
            copy.wait()

    pl.when(apart)(lambda: write(near))
    pl.when(jnp.logical_not(apart))(lambda: write(far))


def sum_kernel(kept, received, *refs):
    total = refs[-1]
    total[...] = (kept[...] + received[...].astype(jnp.float32)).astype(jnp.bfloat16)


def estimate(us):
    return pl.CostEstimate(
        flops=int(us * 1e9), bytes_accessed=int(us * 3.5e6), transcendentals=0
    )


def gate(arrays, tokens):
    n = len(arrays)
    return pl.pallas_call(
        lambda *refs: None,
        out_shape=[jax.ShapeDtypeStruct(x.shape, x.dtype) for x in arrays],
        in_specs=[ANY] * (n + len(tokens)),
        out_specs=[ANY] * n,
        input_output_aliases={i: i for i in range(n)},
        compiler_params=params(1),
        cost_estimate=estimate(0.5),
        name="gate",
    )(*arrays, *tokens)


def chained(queries, out_grad, owner, store_row, store, norm_gain, w_key, w_value):
    stored, length, width = store.shape
    spans, neighbours_per = owner.shape
    peers, groups = lax.axis_size("dp"), lax.axis_size("mp")
    chain = peers // 2
    tokens = queries.shape[0]
    rows = stored * length
    features = w_key.shape[0]
    position, m = lax.axis_index("dp"), lax.axis_index("mp")
    place = jnp.stack([position // 2, position % 2, m]).astype(jnp.int32)

    def held(x):
        return pltpu.with_memory_space_constraint(x, pltpu.HBM)

    def along(x, r):
        return lax.ppermute(x, "dp", [(i, i ^ (2 * r)) for i in range(peers)])

    def hop(x, pairs):
        return lax.ppermute(
            x, "dp", [(2 * i + y, 2 * j + y) for i, j in pairs for y in range(2)]
        )

    def across(x):
        return lax.ppermute(x, "dp", [(i, i ^ 1) for i in range(peers)])

    def beside(x, q):
        return lax.ppermute(x, "mp", [(i, i ^ q) for i in range(groups)])

    *packed, mine = pl.pallas_call(
        functools.partial(pack_kernel, chain, stored),
        out_shape=[
            jax.ShapeDtypeStruct((2 * tokens + spans * neighbours_per, HEAD), queries.dtype)
        ] * chain
        + [jax.ShapeDtypeStruct((rows + TILE, width), store.dtype)],
        in_specs=[SMEM] * 3 + [HBM] * 3 + [VMEM],
        out_specs=[VMEM] * (chain + 1),
        scratch_shapes=[pltpu.SemaphoreType.DMA((chain, 2)), pltpu.SemaphoreType.DMA],
        compiler_params=params(8),
        cost_estimate=estimate(1),
        name="pack",
    )(
        place,
        held(owner.T),
        held(store_row.T),
        held(queries),
        held(out_grad),
        held(store.reshape(rows, width)),
        held(norm_gain),
    )
    arrived = [beside(mine, q) for q in range(2, groups, 2)]
    swapped = beside(mine, 1)
    asked = [packed[0]] + [along(packed[r], r) for r in range(1, chain - 1)]
    *arrived, late = gate(arrived + [packed[chain - 1]], asked[1:])
    asked.append(along(late, chain - 1))
    states = [mine, swapped]
    for x in arrived:
        states += [x, beside(x, 1)]

    *encoded, normed_own = pl.pallas_call(
        functools.partial(project_kernel, chain, features),
        out_shape=[jax.ShapeDtypeStruct((rows, 2 * HEAD), jnp.bfloat16)] * chain
        + [jax.ShapeDtypeStruct((rows, width), jnp.bfloat16)],
        in_specs=[SMEM, HBM, HBM] + [VMEM] * groups,
        out_specs=[VMEM] * (chain + 1),
        scratch_shapes=[
            pltpu.VMEM((rows, features), jnp.bfloat16),
            pltpu.VMEM((chain, features, 2 * HEAD), jnp.bfloat16),
            pltpu.SemaphoreType.DMA((chain, 2)),
        ],
        compiler_params=params(24),
        cost_estimate=estimate(6),
        name="project",
    )(place, held(w_key), held(w_value), *states)

    near = [encoded[0]] + [along(encoded[r], r) for r in range(1, chain)]
    far = [across(x) for x in near]

    (normed_own,) = gate([normed_own], near)
    turned = lax.ppermute(
        normed_own,
        ("dp", "mp"),
        [
            (i * groups + j, (i ^ (2 * MASKS[j])) * groups + j)
            for i in range(peers)
            for j in range(groups)
        ],
    )

    side_by_side = (chain, spans // 2, neighbours_per * length, 2 * tokens // spans)
    *given, again, kept, sent = pl.pallas_call(
        functools.partial(attend_kernel, chain, spans, stored, length),
        out_shape=[jax.ShapeDtypeStruct((2, tokens, HEAD), queries.dtype)] * (chain + 1)
        + [
            jax.ShapeDtypeStruct((chain, rows, 2 * HEAD), jnp.float32),
            jax.ShapeDtypeStruct((chain, rows, 2 * HEAD), jnp.bfloat16),
        ],
        in_specs=[SMEM] + [VMEM] * (3 * chain),
        out_specs=[VMEM] * (chain + 3),
        scratch_shapes=[
            pltpu.VMEM((peers * stored, length, 2 * HEAD), jnp.bfloat16),
            pltpu.VMEM((peers * stored, length, 2 * HEAD), jnp.float32),
            pltpu.VMEM(side_by_side, jnp.float32),
            pltpu.VMEM(side_by_side, jnp.float32),
            pltpu.VMEM(side_by_side, jnp.bfloat16),
            pltpu.VMEM(side_by_side, jnp.bfloat16),
            pltpu.VMEM((chain, spans * neighbours_per, HEAD), jnp.int32),
            pltpu.SMEM((chain, spans * neighbours_per, HEAD), jnp.int32),
            pltpu.SemaphoreType.DMA,
        ],
        compiler_params=params(28),
        cost_estimate=estimate(14),
        name="attend",
    )(place, *asked, *near, *far)

    received = across(sent)
    returned = [given[0]] + [along(given[r], r) for r in range(1, chain - 1)]
    row_grad = pl.pallas_call(
        sum_kernel,
        out_shape=jax.ShapeDtypeStruct((chain, rows, 2 * HEAD), jnp.bfloat16),
        in_specs=[VMEM, VMEM, ANY, ANY, ANY],
        out_specs=VMEM,
        compiler_params=params(8),
        cost_estimate=estimate(1),
        name="sum",
    )(kept, received, returned[1], returned[2], turned)
    middle, outward, ahead = ((1, 2), (2, 1)), ((2, 3), (1, 0)), ((0, 1), (3, 2))
    beyond, inward = along(row_grad, 1), hop(row_grad, middle)
    onward = hop(beyond, middle)
    row_grads = [
        [row_grad],
        [beyond],
        [inward, hop(inward, outward)],
        [onward, hop(onward, outward)],
    ]

    shares = [turned, beside(turned, 1)]
    for q in range(2, groups, 2):
        x = beside(turned, q)
        shares += [x, beside(x, 1)]
    shares = pl.pallas_call(
        turn_kernel,
        out_shape=[jax.ShapeDtypeStruct((2, width // 2, rows), jnp.bfloat16)] * groups,
        in_specs=[VMEM] * groups,
        out_specs=[VMEM] * groups,
        compiler_params=params(8),
        cost_estimate=estimate(0.1),
        name="turn",
    )(*shares)

    def weigh(sources, wants, token):
        types = [jnp.float32 if want else jnp.bfloat16 for want in wants]
        return pl.pallas_call(
            functools.partial(weigh_kernel, chain, wants),
            out_shape=[jax.ShapeDtypeStruct((width // 2, 2 * HEAD), t) for t in types],
            in_specs=[SMEM] + [VMEM] * groups + [ANY] + [VMEM] * len(sources),
            out_specs=[VMEM] * len(wants),
            compiler_params=params(12),
            cost_estimate=estimate(len(wants)),
            name="weigh",
        )(place, *shares, token, *sources)

    (again,) = gate([again], [beyond])
    passing = hop(again, ahead)

    kept, received, token = [], [], place
    for sources in row_grads[:-1]:
        own, other = weigh(sources, (True, False), token)
        kept.append(own)
        received.append(across(other))
        token = received[-2] if len(received) > 1 else own
        if len(kept) == 2:
            late, passing = gate([given[-1], passing], [onward, own])
            returned.append(hop(late, middle))
            passing = hop(passing, middle)
    (other,) = weigh(row_grads[-1], (False,), token)
    received.append(across(other))
    (own,) = weigh(row_grads[-1], (True,), other)
    kept.append(own)
    (passing,) = gate([passing], [other])
    returned.append(hop(passing, outward))
    answers = [jax.ShapeDtypeStruct(queries.shape, queries.dtype)] * 2
    attended, query_grad = pl.pallas_call(
        functools.partial(unpack_kernel, chain),
        out_shape=answers,
        in_specs=[SMEM] + [VMEM] * (chain - 1),
        out_specs=[VMEM] * 2,
        compiler_params=params(8),
        cost_estimate=estimate(2),
        name="unpack",
    )(place, *returned[:chain - 1])
    results = [jax.ShapeDtypeStruct((width // 2, chain * HEAD), jnp.float32)] * 2
    key_grad, value_grad = pl.pallas_call(
        functools.partial(collect_kernel, chain),
        out_shape=results,
        in_specs=[SMEM] + [VMEM] * (2 * chain - 2),
        out_specs=[VMEM] * 2,
        compiler_params=params(12),
        cost_estimate=estimate(2),
        name="collect",
    )(place, *kept[:-1], *received[:-1])
    return pl.pallas_call(
        functools.partial(finish_kernel, chain),
        out_shape=answers + results,
        in_specs=[SMEM] + [VMEM] * 4 + [ANY] * 4,
        out_specs=[ANY] * 4,
        scratch_shapes=[
            pltpu.VMEM((width // 2, 2 * HEAD), jnp.float32),
            pltpu.SemaphoreType.DMA((4,)),
        ],
        input_output_aliases={5 + i: i for i in range(4)},
        compiler_params=params(4),
        cost_estimate=estimate(1),
        name="finish",
    )(
        place,
        kept[-1],
        received[-1],
        *returned[chain - 1:],
        attended,
        query_grad,
        key_grad,
        value_grad,
    )


def gathered(queries, out_grad, owner, store_row, store, norm_gain, w_key, w_value):
    whole_store, whole_gain = (
        lax.all_gather(store, "mp", axis=2, tiled=True),
        lax.all_gather(norm_gain, "mp", axis=0, tiled=True),
    )
    stored, length, model_width = whole_store.shape
    floats = whole_store.astype(jnp.float32)
    scale_rows = lax.rsqrt(jnp.mean(floats * floats, axis=-1, keepdims=True) + epsilon)
    normed = (
        (floats * scale_rows * whole_gain.astype(jnp.float32))
        .astype(jnp.bfloat16)
        .reshape(stored * length, model_width)
    )
    columns_half = w_key.shape[1]
    key_rows = jnp.dot(normed, w_key, preferred_element_type=jnp.float32).astype(jnp.bfloat16)
    value_rows = jnp.dot(normed, w_value, preferred_element_type=jnp.float32).astype(jnp.bfloat16)
    encoded = jnp.concatenate([key_rows, value_rows], axis=1).reshape(
        stored, length, 2 * columns_half
    )
    spans, neighbours_per = owner.shape
    references = spans * neighbours_per
    peer_count = lax.axis_size("dp")
    own_flat = owner.reshape(references)
    row_flat = store_row.reshape(references)
    global_id = own_flat * stored + row_flat
    earlier = jnp.tril(jnp.ones((references, references), jnp.int32), -1)
    everything = lax.all_gather(encoded, "dp", axis=0, tiled=True)
    context = jnp.take(everything, global_id, axis=0)
    head_size = HEAD
    heads_here = columns_half // head_size
    context_all = context.reshape(spans, neighbours_per * length, 2, heads_here, head_size)
    key_ctx = context_all[:, :, 0]
    value_ctx = context_all[:, :, 1]
    tokens = queries.reshape(spans, -1, heads_here, head_size)
    grads_out = out_grad.reshape(spans, -1, heads_here, head_size)
    inverse_root = 1.0 / math.sqrt(head_size)
    scores = (
        jnp.einsum("cqhd,ckhd->chqk", tokens, key_ctx, preferred_element_type=jnp.float32)
        * inverse_root
    )
    probs = jax.nn.softmax(scores, axis=-1)
    probs_low = probs.astype(jnp.bfloat16)
    attended = (
        jnp.einsum("chqk,ckhd->cqhd", probs_low, value_ctx, preferred_element_type=jnp.float32)
        .astype(jnp.bfloat16)
        .reshape(queries.shape)
    )
    prob_grad = jnp.einsum(
        "cqhd,ckhd->chqk", grads_out, value_ctx, preferred_element_type=jnp.float32
    )
    row_delta = jnp.sum(probs * prob_grad, axis=-1, keepdims=True)
    score_grad = (probs * (prob_grad - row_delta)).astype(jnp.bfloat16)
    query_grad = (
        (
            jnp.einsum("chqk,ckhd->cqhd", score_grad, key_ctx, preferred_element_type=jnp.float32)
            * inverse_root
        )
        .astype(jnp.bfloat16)
        .reshape(queries.shape)
    )
    key_grad = (
        jnp.einsum("chqk,cqhd->ckhd", score_grad, tokens, preferred_element_type=jnp.float32)
        * inverse_root
    )
    value_grad = jnp.einsum(
        "chqk,cqhd->ckhd", probs_low, grads_out, preferred_element_type=jnp.float32
    )
    ref_grads = jnp.stack([key_grad, value_grad], axis=2).reshape(
        references, length, 2 * columns_half
    )
    same_id = (global_id[:, None] == global_id[None, :]).astype(jnp.float32)
    first_use = jnp.sum(same_id * earlier.astype(jnp.float32), axis=1) == 0.0
    summed = jnp.einsum("ij,jtc->itc", same_id, ref_grads, precision=lax.Precision.HIGHEST)
    sent_grads = jnp.where(first_use[:, None, None], summed, 0.0).astype(jnp.bfloat16)
    placement_table = (global_id[:, None] == jnp.arange(peer_count * stored)[None, :]).astype(
        jnp.bfloat16
    )
    dense_grads = jnp.einsum(
        "ir,itc->rtc", placement_table, sent_grads, preferred_element_type=jnp.float32
    )
    row_grad = lax.psum_scatter(
        dense_grads.astype(jnp.bfloat16), "dp", scatter_dimension=0, tiled=True
    )
    row_grad_low = row_grad.reshape(stored * length, 2 * columns_half)
    weight_grad = lax.psum_scatter(
        lax.dot_general(
            normed, row_grad_low, (((0,), (0,)), ((), ())), preferred_element_type=jnp.float32
        ).astype(jnp.bfloat16),
        "dp",
        scatter_dimension=0,
        tiled=True,
    ).astype(jnp.float32)
    return (attended, query_grad, weight_grad[:, :columns_half], weight_grad[:, columns_half:])


def solution(mesh):
    in_specs = (
        P("dp", "mp"),
        P("dp", "mp"),
        P("dp", None),
        P("dp", None),
        P("dp", None, "mp"),
        P("mp"),
        P(None, "mp"),
        P(None, "mp"),
    )
    out_specs = (P("dp", "mp"), P("dp", "mp"), P("dp", "mp"), P("dp", "mp"))
    def shards(*args):
        peers, groups = lax.axis_size("dp"), lax.axis_size("mp")
        heads_here = args[6].shape[1] // HEAD
        if peers == 2 * heads_here == 2 * groups == 8:
            return chained(*args)
        return gathered(*args)

    return jax.shard_map(shards, mesh=mesh, in_specs=in_specs, out_specs=out_specs, check_vma=False)
```

```python
import functools
import math

import jax
import jax.numpy as jnp
from jax import lax
from jax.experimental import pallas as pl
from jax.experimental.pallas import tpu as pltpu
from jax.sharding import PartitionSpec as P

HEAD = 128
TILE = 16


epsilon = 1e-06

def params(mebibytes):
    return pltpu.CompilerParams(vmem_limit_bytes=mebibytes * 1024 * 1024)


VMEM = pl.BlockSpec(memory_space=pltpu.VMEM)
SMEM = pl.BlockSpec(memory_space=pltpu.SMEM)
ANY = pl.BlockSpec(memory_space=pl.ANY)
HBM = pl.BlockSpec(memory_space=pltpu.HBM)


def column(head):
    return pl.ds(pl.multiple_of(head * HEAD, HEAD), HEAD)


def pack_kernel(chain, slots, place, owner, store_row, queries, out_grad, store, gain, *refs):
    packed, (bundle, sems, sem) = refs[:chain], refs[chain:]
    tokens, rows = queries.shape[0], store.shape[0]
    named, spans = owner.shape
    copies = [pltpu.make_async_copy(store, bundle.at[pl.ds(0, rows), :], sem)] + [
        pltpu.make_async_copy(
            source.at[:, column(place[0] ^ r)],
            packed[r].at[pl.ds(side * tokens, tokens), :],
            sems.at[r, side],
        )
        for r in range(chain)
        for side, source in enumerate((queries, out_grad))
    ]
    for copy in copies:
        copy.start()
    bundle[pl.ds(rows, TILE), :] = jnp.broadcast_to(gain[...].reshape(1, store.shape[1]), (TILE, store.shape[1]))
    line = lax.broadcasted_iota(jnp.int32, (spans * named, HEAD), 0)
    block = jnp.zeros((spans * named, HEAD), jnp.int32)
    for i in range(spans * named):
        spot = (i % named, i // named)
        block = jnp.where(line == i, owner[spot] * slots + store_row[spot], block)
    block = block.astype(jnp.float32).astype(jnp.bfloat16)
    for r in range(chain):
        packed[r][pl.ds(2 * tokens, spans * named), :] = block
    for copy in copies:
        copy.wait()


def unpack_kernel(chain, place, *refs):
    parts, (attended, query_grad) = refs[:chain - 1], refs[chain - 1:]
    for r, part in enumerate(parts):
        attended[:, column(place[0] ^ r)] = part[0]
        query_grad[:, column(place[0] ^ r)] = part[1]


MASKS = (0, 3, 1, 2)


def mask(m):
    return sum(jnp.where(m == i, x, 0) for i, x in enumerate(MASKS))


def project_kernel(chain, features, place, w_key, w_value, *refs):
    shards = len(refs) - chain - 4
    states, refs = refs[:shards], refs[shards:]
    encoded, (normed_own, normed, weights, sems) = refs[:chain], refs[chain:]
    copies = [
        pltpu.make_async_copy(
            source.at[:, column(place[0] ^ r)],
            weights.at[r, :, pl.ds(side * HEAD, HEAD)],
            sems.at[r, side],
        )
        for r in range(chain)
        for side, source in enumerate((w_key, w_value))
    ]
    for copy in copies:
        copy.start()
    m = place[2]
    rows, width = normed_own.shape
    gain = [x[pl.ds(rows, TILE), :].astype(jnp.float32) for x in states]

    def norm_tile(i, carry):
        part = pl.ds(pl.multiple_of(i * TILE, TILE), TILE)
        square = jnp.zeros((TILE, 1), jnp.float32)
        for x in states:
            floats = x[part, :].astype(jnp.float32)
            square += jnp.sum(floats * floats, axis=-1, keepdims=True)
        scale = lax.rsqrt(square / features + epsilon)
        for q, x in enumerate(states):
            low = (x[part, :].astype(jnp.float32) * scale * gain[q]).astype(jnp.bfloat16)
            normed[part, pl.ds(pl.multiple_of((m ^ q) * width, width), width)] = low
        return carry

    lax.fori_loop(0, rows // TILE, norm_tile, 0, unroll=2)
    block = place[0] ^ mask(m)
    normed_own[...] = normed[:, pl.ds(pl.multiple_of(block * width, width), width)]
    for r in range(chain):
        copies[2 * r].wait()
        copies[2 * r + 1].wait()
        encoded[r][...] = jnp.dot(
            normed[...], weights[r], preferred_element_type=jnp.float32
        ).astype(jnp.bfloat16)


def dot_t(left, right):
    return lax.dot_general(
        left, right, (((1,), (1,)), ((), ())), preferred_element_type=jnp.float32
    )


def dot_0(left, right):
    return lax.dot_general(
        left, right, (((0,), (0,)), ((), ())), preferred_element_type=jnp.float32
    )


def attend_kernel(chain, spans, slots, length, place, *refs):
    asked, refs = refs[:chain], refs[chain:]
    near, far, refs = refs[:chain], refs[chain:2 * chain], refs[2 * chain:]
    given, again, refs = refs[:chain], refs[chain], refs[chain + 1:]
    kept, sent, context, grads, scores, prob_grads, lows, score_grads, lines, ids, sem = refs
    a, y = place[0], place[1]
    tokens = given[0].shape[1]
    span_len = tokens // spans
    pairs = spans // 2
    width = 2 * span_len
    named = 2 * spans
    inverse_root = 1.0 / math.sqrt(HEAD)
    for r in range(chain):
        lines[r] = asked[r][pl.ds(2 * tokens, named), :].astype(jnp.float32).astype(jnp.int32)
    copy = pltpu.make_async_copy(lines, ids, sem)
    copy.start()
    for r in range(chain):
        first = (a ^ r) * 2 * slots
        for s in range(slots):
            context[first + y * slots + s] = near[r][pl.ds(s * length, length), :]
            context[first + (1 - y) * slots + s] = far[r][pl.ds(s * length, length), :]
    grads[...] = jnp.zeros_like(grads)
    copy.wait()

    def fetch(r, c):
        rows = [[ids[r, 4 * c + 2 * h + n, 0] for n in range(2)] for h in range(2)]
        key = [jnp.concatenate([context[i, :, :HEAD] for i in row], axis=0) for row in rows]
        value = [jnp.concatenate([context[i, :, HEAD:] for i in row], axis=0) for row in rows]
        query = asked[r][pl.ds(pl.multiple_of(c * width, width), width), :]
        grad = asked[r][pl.ds(pl.multiple_of(tokens + c * width, width), width), :]
        return rows, key, value, query, grad

    def products(c, carry):
        first = lax.broadcasted_iota(jnp.int32, (2 * length, width), 1) < span_len
        for r in range(chain):
            rows, key, value, query, grad = fetch(r, c)
            scores[r, c] = jnp.where(first, dot_t(key[0], query), dot_t(key[1], query))
            prob_grads[r, c] = jnp.where(first, dot_t(value[0], grad), dot_t(value[1], grad))
        return carry

    lax.fori_loop(0, pairs, products, 0)

    def soften(c, carry):
        for r in range(chain):
            score = scores[r, c] * inverse_root
            powers = jnp.exp(score - jnp.max(score, axis=0, keepdims=True))
            probs = powers * (1.0 / jnp.sum(powers, axis=0, keepdims=True))
            lows[r, c] = probs.astype(jnp.bfloat16)
            prob_grad = prob_grads[r, c]
            delta = jnp.sum(probs * prob_grad, axis=0, keepdims=True)
            score_grads[r, c] = (probs * (prob_grad - delta)).astype(jnp.bfloat16)
        return carry

    lax.fori_loop(0, pairs, soften, 0)

    def results(c, carry):
        upper = lax.broadcasted_iota(jnp.int32, (width, HEAD), 0) < span_len
        both = pl.ds(pl.multiple_of(c * width, width), width)
        for r in range(chain):
            rows, key, value, query, grad = fetch(r, c)
            low, score_grad = lows[r, c], score_grads[r, c]
            for h in range(2):
                mine = upper if h == 0 else jnp.logical_not(upper)
                key_part = jnp.dot(
                    score_grad,
                    jnp.where(mine, query, jnp.zeros_like(query)),
                    preferred_element_type=jnp.float32,
                )
                value_part = jnp.dot(
                    low,
                    jnp.where(mine, grad, jnp.zeros_like(grad)),
                    preferred_element_type=jnp.float32,
                )
                for n in range(2):
                    part = slice(n * length, (n + 1) * length)
                    grads[rows[h][n], :, :HEAD] += key_part[part]
                    grads[rows[h][n], :, HEAD:] += value_part[part]
            attended = jnp.where(upper, dot_0(low, value[0]), dot_0(low, value[1]))
            query_grad = jnp.where(upper, dot_0(score_grad, key[0]), dot_0(score_grad, key[1]))
            given[r][0, both, :] = attended.astype(jnp.bfloat16)
            given[r][1, both, :] = (query_grad * inverse_root).astype(jnp.bfloat16)
        return carry

    lax.fori_loop(0, pairs, results, 0)
    again[:, pl.ds(0, tokens), :] = given[chain - 1][...]
    again[:, pl.ds(tokens, TILE), :] = jnp.zeros((2, TILE, HEAD), jnp.bfloat16)
    for member in range(chain):
        for s in range(slots):
            part = pl.ds(s * length, length)
            own = member * 2 * slots + y * slots + s
            other = member * 2 * slots + (1 - y) * slots + s
            kept[member, part, :HEAD] = grads[own, :, :HEAD] * inverse_root
            kept[member, part, HEAD:] = grads[own, :, HEAD:]
            sent[member, part, :HEAD] = (grads[other, :, :HEAD] * inverse_root).astype(jnp.bfloat16)
            sent[member, part, HEAD:] = grads[other, :, HEAD:].astype(jnp.bfloat16)


def turn_kernel(*refs):
    count = len(refs) // 2
    for share, result in zip(refs[:count], refs[count:]):
        half = result.shape[1]
        for side in range(2):
            result[side] = share[:, side * half:(side + 1) * half].T


def inner(place):
    return (place[0] == 1) | (place[0] == 2)


def weigh_kernel(chain, wants, place, *refs):
    shares, refs = refs[:chain], refs[chain + 1:]
    sources, targets = refs[:-len(wants)], refs[-len(wants):]

    def multiply(row_grad):
        for want, target in zip(wants, targets):
            half = place[1] if want else 1 - place[1]
            total = sum(
                jnp.dot(
                    shares[q][half],
                    row_grad[place[0] ^ mask(place[2] ^ q)],
                    preferred_element_type=jnp.float32,
                )
                for q in range(chain)
            )
            target[...] = total.astype(target.dtype)

    if len(sources) == 1:
        multiply(sources[0])
    else:
        pl.when(inner(place))(lambda: multiply(sources[0]))
        pl.when(jnp.logical_not(inner(place)))(lambda: multiply(sources[1]))


def collect_kernel(chain, place, *refs):
    count = chain - 1
    kept, received, (key_grad, value_grad) = refs[:count], refs[count:2 * count], refs[2 * count:]
    a = place[0]
    turned = inner(place).astype(jnp.int32)
    for r, head in enumerate((a, a ^ 1, a ^ (2 + turned))):
        total = kept[r][...] + received[r][...].astype(jnp.float32)
        key_grad[:, column(head)] = total[:, :HEAD]
        value_grad[:, column(head)] = total[:, HEAD:]


def finish_kernel(chain, place, kept, received, near, far, *refs):
    targets, (total, sems) = refs[4:8], refs[8:]
    apart = inner(place)

    def write(part):
        copies = [
            pltpu.make_async_copy(
                part.at[side, pl.ds(0, targets[side].shape[0]), :],
                targets[side].at[:, column(place[0] ^ (chain - 1))],
                sems.at[side],
            )
            for side in range(2)
        ]
        for copy in copies:
            copy.start()
        total[...] = kept[...] + received[...].astype(jnp.float32)
        copies += [
            pltpu.make_async_copy(
                total.at[:, pl.ds(side * HEAD, HEAD)],
                targets[2 + side].at[:, column(place[0] ^ (3 - apart.astype(jnp.int32)))],
                sems.at[2 + side],
            )
            for side in range(2)
        ]
        for copy in copies[2:]:
            copy.start()
        for copy in copies:
            copy.wait()

    pl.when(apart)(lambda: write(near))
    pl.when(jnp.logical_not(apart))(lambda: write(far))


def sum_kernel(kept, received, *refs):
    total = refs[-1]
    total[...] = (kept[...] + received[...].astype(jnp.float32)).astype(jnp.bfloat16)


def estimate(us):
    return pl.CostEstimate(
        flops=int(us * 1e9), bytes_accessed=int(us * 3.5e6), transcendentals=0
    )


def gate(arrays, tokens):
    n = len(arrays)
    return pl.pallas_call(
        lambda *refs: None,
        out_shape=[jax.ShapeDtypeStruct(x.shape, x.dtype) for x in arrays],
        in_specs=[ANY] * (n + len(tokens)),
        out_specs=[ANY] * n,
        input_output_aliases={i: i for i in range(n)},
        compiler_params=params(1),
        cost_estimate=estimate(0.5),
        name="gate",
    )(*arrays, *tokens)


def chained(queries, out_grad, owner, store_row, store, norm_gain, w_key, w_value):
    stored, length, width = store.shape
    spans, neighbours_per = owner.shape
    peers, groups = lax.axis_size("dp"), lax.axis_size("mp")
    chain = peers // 2
    tokens = queries.shape[0]
    rows = stored * length
    features = w_key.shape[0]
    position, m = lax.axis_index("dp"), lax.axis_index("mp")
    place = jnp.stack([position // 2, position % 2, m]).astype(jnp.int32)

    def held(x):
        return pltpu.with_memory_space_constraint(x, pltpu.HBM)

    def along(x, r):
        return lax.ppermute(x, "dp", [(i, i ^ (2 * r)) for i in range(peers)])

    def hop(x, pairs):
        return lax.ppermute(
            x, "dp", [(2 * i + y, 2 * j + y) for i, j in pairs for y in range(2)]
        )

    def across(x):
        return lax.ppermute(x, "dp", [(i, i ^ 1) for i in range(peers)])

    def beside(x, q):
        return lax.ppermute(x, "mp", [(i, i ^ q) for i in range(groups)])

    *packed, mine = pl.pallas_call(
        functools.partial(pack_kernel, chain, stored),
        out_shape=[
            jax.ShapeDtypeStruct((2 * tokens + spans * neighbours_per, HEAD), queries.dtype)
        ] * chain
        + [jax.ShapeDtypeStruct((rows + TILE, width), store.dtype)],
        in_specs=[SMEM] * 3 + [HBM] * 3 + [VMEM],
        out_specs=[VMEM] * (chain + 1),
        scratch_shapes=[pltpu.SemaphoreType.DMA((chain, 2)), pltpu.SemaphoreType.DMA],
        compiler_params=params(8),
        cost_estimate=estimate(1),
        name="pack",
    )(
        place,
        held(owner.T),
        held(store_row.T),
        held(queries),
        held(out_grad),
        held(store.reshape(rows, width)),
        held(norm_gain),
    )
    arrived = [beside(mine, q) for q in range(2, groups, 2)]
    swapped = beside(mine, 1)
    asked = [packed[0]] + [along(packed[r], r) for r in range(1, chain - 1)]
    *arrived, late = gate(arrived + [packed[chain - 1]], asked[1:])
    asked.append(along(late, chain - 1))
    states = [mine, swapped]
    for x in arrived:
        states += [x, beside(x, 1)]

    *encoded, normed_own = pl.pallas_call(
        functools.partial(project_kernel, chain, features),
        out_shape=[jax.ShapeDtypeStruct((rows, 2 * HEAD), jnp.bfloat16)] * chain
        + [jax.ShapeDtypeStruct((rows, width), jnp.bfloat16)],
        in_specs=[SMEM, HBM, HBM] + [VMEM] * groups,
        out_specs=[VMEM] * (chain + 1),
        scratch_shapes=[
            pltpu.VMEM((rows, features), jnp.bfloat16),
            pltpu.VMEM((chain, features, 2 * HEAD), jnp.bfloat16),
            pltpu.SemaphoreType.DMA((chain, 2)),
        ],
        compiler_params=params(24),
        cost_estimate=estimate(6),
        name="project",
    )(place, held(w_key), held(w_value), *states)

    near = [encoded[0]] + [along(encoded[r], r) for r in range(1, chain)]
    far = [across(x) for x in near]

    (normed_own,) = gate([normed_own], near)
    turned = lax.ppermute(
        normed_own,
        ("dp", "mp"),
        [
            (i * groups + j, (i ^ (2 * MASKS[j])) * groups + j)
            for i in range(peers)
            for j in range(groups)
        ],
    )

    side_by_side = (chain, spans // 2, neighbours_per * length, 2 * tokens // spans)
    *given, again, kept, sent = pl.pallas_call(
        functools.partial(attend_kernel, chain, spans, stored, length),
        out_shape=[jax.ShapeDtypeStruct((2, tokens, HEAD), queries.dtype)] * chain
        + [jax.ShapeDtypeStruct((2, tokens + TILE, HEAD), queries.dtype)]
        + [
            jax.ShapeDtypeStruct((chain, rows, 2 * HEAD), jnp.float32),
            jax.ShapeDtypeStruct((chain, rows, 2 * HEAD), jnp.bfloat16),
        ],
        in_specs=[SMEM] + [VMEM] * (3 * chain),
        out_specs=[VMEM] * (chain + 3),
        scratch_shapes=[
            pltpu.VMEM((peers * stored, length, 2 * HEAD), jnp.bfloat16),
            pltpu.VMEM((peers * stored, length, 2 * HEAD), jnp.float32),
            pltpu.VMEM(side_by_side, jnp.float32),
            pltpu.VMEM(side_by_side, jnp.float32),
            pltpu.VMEM(side_by_side, jnp.bfloat16),
            pltpu.VMEM(side_by_side, jnp.bfloat16),
            pltpu.VMEM((chain, spans * neighbours_per, HEAD), jnp.int32),
            pltpu.SMEM((chain, spans * neighbours_per, HEAD), jnp.int32),
            pltpu.SemaphoreType.DMA,
        ],
        compiler_params=params(28),
        cost_estimate=estimate(14),
        name="attend",
    )(place, *asked, *near, *far)

    received = across(sent)
    returned = [given[0]] + [along(given[r], r) for r in range(1, chain - 1)]
    row_grad = pl.pallas_call(
        sum_kernel,
        out_shape=jax.ShapeDtypeStruct((chain, rows, 2 * HEAD), jnp.bfloat16),
        in_specs=[VMEM, VMEM, ANY, ANY, ANY],
        out_specs=VMEM,
        compiler_params=params(8),
        cost_estimate=estimate(1),
        name="sum",
    )(kept, received, returned[1], returned[2], turned)
    middle, outward, ahead = ((1, 2), (2, 1)), ((2, 3), (1, 0)), ((0, 1), (3, 2))
    beyond, inward = along(row_grad, 1), hop(row_grad, middle)
    onward = hop(beyond, middle)
    row_grads = [
        [row_grad],
        [beyond],
        [inward, hop(inward, outward)],
        [onward, hop(onward, outward)],
    ]

    shares = [turned, beside(turned, 1)]
    for q in range(2, groups, 2):
        x = beside(turned, q)
        shares += [x, beside(x, 1)]
    shares = pl.pallas_call(
        turn_kernel,
        out_shape=[jax.ShapeDtypeStruct((2, width // 2, rows), jnp.bfloat16)] * groups,
        in_specs=[VMEM] * groups,
        out_specs=[VMEM] * groups,
        compiler_params=params(8),
        cost_estimate=estimate(0.1),
        name="turn",
    )(*shares)

    def weigh(sources, wants, token):
        types = [jnp.float32 if want else jnp.bfloat16 for want in wants]
        return pl.pallas_call(
            functools.partial(weigh_kernel, chain, wants),
            out_shape=[jax.ShapeDtypeStruct((width // 2, 2 * HEAD), t) for t in types],
            in_specs=[SMEM] + [VMEM] * groups + [ANY] + [VMEM] * len(sources),
            out_specs=[VMEM] * len(wants),
            compiler_params=params(12),
            cost_estimate=estimate(len(wants)),
            name="weigh",
        )(place, *shares, token, *sources)

    (again,) = gate([again], [beyond])
    passing = hop(again, ahead)

    kept, received, token = [], [], place
    for sources in row_grads[:-1]:
        own, other = weigh(sources, (True, False), token)
        kept.append(own)
        received.append(across(other))
        token = received[-2] if len(received) > 1 else own
        if len(kept) == 2:
            (passing,) = gate([passing], [onward, own])
            passing = hop(passing, middle)
    (passing,) = gate([passing], [received[1]])
    (other,) = weigh(row_grads[-1], (False,), passing)
    far = hop(passing, outward)
    (late,) = gate([given[-1]], [other])
    near = hop(late, middle)
    received.append(across(other))
    (own,) = weigh(row_grads[-1], (True,), other)
    kept.append(own)
    answers = [jax.ShapeDtypeStruct(queries.shape, queries.dtype)] * 2
    attended, query_grad = pl.pallas_call(
        functools.partial(unpack_kernel, chain),
        out_shape=answers,
        in_specs=[SMEM] + [VMEM] * (chain - 1),
        out_specs=[VMEM] * 2,
        compiler_params=params(8),
        cost_estimate=estimate(2),
        name="unpack",
    )(place, *returned[:chain - 1])
    results = [jax.ShapeDtypeStruct((width // 2, chain * HEAD), jnp.float32)] * 2
    key_grad, value_grad = pl.pallas_call(
        functools.partial(collect_kernel, chain),
        out_shape=results,
        in_specs=[SMEM] + [VMEM] * (2 * chain - 2),
        out_specs=[VMEM] * 2,
        compiler_params=params(12),
        cost_estimate=estimate(2),
        name="collect",
    )(place, *kept[:-1], *received[:-1])
    return pl.pallas_call(
        functools.partial(finish_kernel, chain),
        out_shape=answers + results,
        in_specs=[SMEM] + [VMEM] * 4 + [ANY] * 4,
        out_specs=[ANY] * 4,
        scratch_shapes=[
            pltpu.VMEM((width // 2, 2 * HEAD), jnp.float32),
            pltpu.SemaphoreType.DMA((4,)),
        ],
        input_output_aliases={5 + i: i for i in range(4)},
        compiler_params=params(4),
        cost_estimate=estimate(1),
        name="finish",
    )(
        place,
        kept[-1],
        received[-1],
        near,
        far,
        attended,
        query_grad,
        key_grad,
        value_grad,
    )


def gathered(queries, out_grad, owner, store_row, store, norm_gain, w_key, w_value):
    whole_store, whole_gain = (
        lax.all_gather(store, "mp", axis=2, tiled=True),
        lax.all_gather(norm_gain, "mp", axis=0, tiled=True),
    )
    stored, length, model_width = whole_store.shape
    floats = whole_store.astype(jnp.float32)
    scale_rows = lax.rsqrt(jnp.mean(floats * floats, axis=-1, keepdims=True) + epsilon)
    normed = (
        (floats * scale_rows * whole_gain.astype(jnp.float32))
        .astype(jnp.bfloat16)
        .reshape(stored * length, model_width)
    )
    columns_half = w_key.shape[1]
    key_rows = jnp.dot(normed, w_key, preferred_element_type=jnp.float32).astype(jnp.bfloat16)
    value_rows = jnp.dot(normed, w_value, preferred_element_type=jnp.float32).astype(jnp.bfloat16)
    encoded = jnp.concatenate([key_rows, value_rows], axis=1).reshape(
        stored, length, 2 * columns_half
    )
    spans, neighbours_per = owner.shape
    references = spans * neighbours_per
    peer_count = lax.axis_size("dp")
    own_flat = owner.reshape(references)
    row_flat = store_row.reshape(references)
    global_id = own_flat * stored + row_flat
    earlier = jnp.tril(jnp.ones((references, references), jnp.int32), -1)
    everything = lax.all_gather(encoded, "dp", axis=0, tiled=True)
    context = jnp.take(everything, global_id, axis=0)
    head_size = HEAD
    heads_here = columns_half // head_size
    context_all = context.reshape(spans, neighbours_per * length, 2, heads_here, head_size)
    key_ctx = context_all[:, :, 0]
    value_ctx = context_all[:, :, 1]
    tokens = queries.reshape(spans, -1, heads_here, head_size)
    grads_out = out_grad.reshape(spans, -1, heads_here, head_size)
    inverse_root = 1.0 / math.sqrt(head_size)
    scores = (
        jnp.einsum("cqhd,ckhd->chqk", tokens, key_ctx, preferred_element_type=jnp.float32)
        * inverse_root
    )
    probs = jax.nn.softmax(scores, axis=-1)
    probs_low = probs.astype(jnp.bfloat16)
    attended = (
        jnp.einsum("chqk,ckhd->cqhd", probs_low, value_ctx, preferred_element_type=jnp.float32)
        .astype(jnp.bfloat16)
        .reshape(queries.shape)
    )
    prob_grad = jnp.einsum(
        "cqhd,ckhd->chqk", grads_out, value_ctx, preferred_element_type=jnp.float32
    )
    row_delta = jnp.sum(probs * prob_grad, axis=-1, keepdims=True)
    score_grad = (probs * (prob_grad - row_delta)).astype(jnp.bfloat16)
    query_grad = (
        (
            jnp.einsum("chqk,ckhd->cqhd", score_grad, key_ctx, preferred_element_type=jnp.float32)
            * inverse_root
        )
        .astype(jnp.bfloat16)
        .reshape(queries.shape)
    )
    key_grad = (
        jnp.einsum("chqk,cqhd->ckhd", score_grad, tokens, preferred_element_type=jnp.float32)
        * inverse_root
    )
    value_grad = jnp.einsum(
        "chqk,cqhd->ckhd", probs_low, grads_out, preferred_element_type=jnp.float32
    )
    ref_grads = jnp.stack([key_grad, value_grad], axis=2).reshape(
        references, length, 2 * columns_half
    )
    same_id = (global_id[:, None] == global_id[None, :]).astype(jnp.float32)
    first_use = jnp.sum(same_id * earlier.astype(jnp.float32), axis=1) == 0.0
    summed = jnp.einsum("ij,jtc->itc", same_id, ref_grads, precision=lax.Precision.HIGHEST)
    sent_grads = jnp.where(first_use[:, None, None], summed, 0.0).astype(jnp.bfloat16)
    placement_table = (global_id[:, None] == jnp.arange(peer_count * stored)[None, :]).astype(
        jnp.bfloat16
    )
    dense_grads = jnp.einsum(
        "ir,itc->rtc", placement_table, sent_grads, preferred_element_type=jnp.float32
    )
    row_grad = lax.psum_scatter(
        dense_grads.astype(jnp.bfloat16), "dp", scatter_dimension=0, tiled=True
    )
    row_grad_low = row_grad.reshape(stored * length, 2 * columns_half)
    weight_grad = lax.psum_scatter(
        lax.dot_general(
            normed, row_grad_low, (((0,), (0,)), ((), ())), preferred_element_type=jnp.float32
        ).astype(jnp.bfloat16),
        "dp",
        scatter_dimension=0,
        tiled=True,
    ).astype(jnp.float32)
    return (attended, query_grad, weight_grad[:, :columns_half], weight_grad[:, columns_half:])


def solution(mesh):
    in_specs = (
        P("dp", "mp"),
        P("dp", "mp"),
        P("dp", None),
        P("dp", None),
        P("dp", None, "mp"),
        P("mp"),
        P(None, "mp"),
        P(None, "mp"),
    )
    out_specs = (P("dp", "mp"), P("dp", "mp"), P("dp", "mp"), P("dp", "mp"))
    def shards(*args):
        peers, groups = lax.axis_size("dp"), lax.axis_size("mp")
        heads_here = args[6].shape[1] // HEAD
        if peers == 2 * heads_here == 2 * groups == 8:
            return chained(*args)
        return gathered(*args)

    return jax.shard_map(shards, mesh=mesh, in_specs=in_specs, out_specs=out_specs, check_vma=False)
```

```python
import functools
import math

import jax
import jax.numpy as jnp
from jax import lax
from jax.experimental import pallas as pl
from jax.experimental.pallas import tpu as pltpu
from jax.sharding import PartitionSpec as P

HEAD = 128
TILE = 16


epsilon = 1e-06

def params(mebibytes):
    return pltpu.CompilerParams(vmem_limit_bytes=mebibytes * 1024 * 1024)


VMEM = pl.BlockSpec(memory_space=pltpu.VMEM)
SMEM = pl.BlockSpec(memory_space=pltpu.SMEM)
ANY = pl.BlockSpec(memory_space=pl.ANY)
HBM = pl.BlockSpec(memory_space=pltpu.HBM)


def column(head):
    return pl.ds(pl.multiple_of(head * HEAD, HEAD), HEAD)


def pack_kernel(chain, slots, place, owner, store_row, queries, out_grad, store, gain, *refs):
    packed, (bundle, sems, sem) = refs[:chain], refs[chain:]
    tokens, rows = queries.shape[0], store.shape[0]
    named, spans = owner.shape
    copies = [pltpu.make_async_copy(store, bundle.at[pl.ds(0, rows), :], sem)] + [
        pltpu.make_async_copy(
            source.at[:, column(place[0] ^ r)],
            packed[r].at[pl.ds(side * tokens, tokens), :],
            sems.at[r, side],
        )
        for r in range(chain)
        for side, source in enumerate((queries, out_grad))
    ]
    for copy in copies:
        copy.start()
    bundle[pl.ds(rows, TILE), :] = jnp.broadcast_to(gain[...].reshape(1, store.shape[1]), (TILE, store.shape[1]))
    line = lax.broadcasted_iota(jnp.int32, (spans * named, HEAD), 0)
    block = jnp.zeros((spans * named, HEAD), jnp.int32)
    for i in range(spans * named):
        spot = (i % named, i // named)
        block = jnp.where(line == i, owner[spot] * slots + store_row[spot], block)
    block = block.astype(jnp.float32).astype(jnp.bfloat16)
    for r in range(chain):
        packed[r][pl.ds(2 * tokens, spans * named), :] = block
    for copy in copies:
        copy.wait()


def unpack_kernel(chain, place, *refs):
    parts, (attended, query_grad) = refs[:chain - 1], refs[chain - 1:]
    for r, part in enumerate(parts):
        attended[:, column(place[0] ^ r)] = part[0]
        query_grad[:, column(place[0] ^ r)] = part[1]


MASKS = (0, 3, 1, 2)


def mask(m):
    return sum(jnp.where(m == i, x, 0) for i, x in enumerate(MASKS))


def project_kernel(chain, features, place, w_key, w_value, *refs):
    shards = len(refs) - chain - 4
    states, refs = refs[:shards], refs[shards:]
    encoded, (normed_own, normed, weights, sems) = refs[:chain], refs[chain:]
    copies = [
        pltpu.make_async_copy(
            source.at[:, column(place[0] ^ r)],
            weights.at[r, :, pl.ds(side * HEAD, HEAD)],
            sems.at[r, side],
        )
        for r in range(chain)
        for side, source in enumerate((w_key, w_value))
    ]
    for copy in copies:
        copy.start()
    m = place[2]
    rows, width = normed_own.shape
    gain = [x[pl.ds(rows, TILE), :].astype(jnp.float32) for x in states]

    def norm_tile(i, carry):
        part = pl.ds(pl.multiple_of(i * TILE, TILE), TILE)
        square = jnp.zeros((TILE, 1), jnp.float32)
        for x in states:
            floats = x[part, :].astype(jnp.float32)
            square += jnp.sum(floats * floats, axis=-1, keepdims=True)
        scale = lax.rsqrt(square / features + epsilon)
        for q, x in enumerate(states):
            low = (x[part, :].astype(jnp.float32) * scale * gain[q]).astype(jnp.bfloat16)
            normed[part, pl.ds(pl.multiple_of((m ^ q) * width, width), width)] = low
        return carry

    lax.fori_loop(0, rows // TILE, norm_tile, 0, unroll=2)
    block = place[0] ^ mask(m)
    normed_own[...] = normed[:, pl.ds(pl.multiple_of(block * width, width), width)]
    for r in range(chain):
        copies[2 * r].wait()
        copies[2 * r + 1].wait()
        encoded[r][...] = jnp.dot(
            normed[...], weights[r], preferred_element_type=jnp.float32
        ).astype(jnp.bfloat16)


def dot_t(left, right):
    return lax.dot_general(
        left, right, (((1,), (1,)), ((), ())), preferred_element_type=jnp.float32
    )


def dot_0(left, right):
    return lax.dot_general(
        left, right, (((0,), (0,)), ((), ())), preferred_element_type=jnp.float32
    )


def attend_kernel(chain, spans, slots, length, place, *refs):
    asked, refs = refs[:chain], refs[chain:]
    near, far, refs = refs[:chain], refs[chain:2 * chain], refs[2 * chain:]
    given, again, refs = refs[:chain], refs[chain], refs[chain + 1:]
    kept, sent, context, grads, scores, prob_grads, lows, score_grads, lines, ids, sem = refs
    a, y = place[0], place[1]
    tokens = given[0].shape[1]
    span_len = tokens // spans
    pairs = spans // 2
    width = 2 * span_len
    named = 2 * spans
    inverse_root = 1.0 / math.sqrt(HEAD)
    for r in range(chain):
        lines[r] = asked[r][pl.ds(2 * tokens, named), :].astype(jnp.float32).astype(jnp.int32)
    copy = pltpu.make_async_copy(lines, ids, sem)
    copy.start()
    for r in range(chain):
        first = (a ^ r) * 2 * slots
        for s in range(slots):
            context[first + y * slots + s] = near[r][pl.ds(s * length, length), :]
            context[first + (1 - y) * slots + s] = far[r][pl.ds(s * length, length), :]
    grads[...] = jnp.zeros_like(grads)
    copy.wait()

    def fetch(r, c):
        rows = [[ids[r, 4 * c + 2 * h + n, 0] for n in range(2)] for h in range(2)]
        key = [jnp.concatenate([context[i, :, :HEAD] for i in row], axis=0) for row in rows]
        value = [jnp.concatenate([context[i, :, HEAD:] for i in row], axis=0) for row in rows]
        query = asked[r][pl.ds(pl.multiple_of(c * width, width), width), :]
        grad = asked[r][pl.ds(pl.multiple_of(tokens + c * width, width), width), :]
        return rows, key, value, query, grad

    def products(c, carry):
        first = lax.broadcasted_iota(jnp.int32, (2 * length, width), 1) < span_len
        for r in range(chain):
            rows, key, value, query, grad = fetch(r, c)
            scores[r, c] = jnp.where(first, dot_t(key[0], query), dot_t(key[1], query))
            prob_grads[r, c] = jnp.where(first, dot_t(value[0], grad), dot_t(value[1], grad))
        return carry

    lax.fori_loop(0, pairs, products, 0)

    def soften(c, carry):
        for r in range(chain):
            score = scores[r, c] * inverse_root
            powers = jnp.exp(score - jnp.max(score, axis=0, keepdims=True))
            probs = powers * (1.0 / jnp.sum(powers, axis=0, keepdims=True))
            lows[r, c] = probs.astype(jnp.bfloat16)
            prob_grad = prob_grads[r, c]
            delta = jnp.sum(probs * prob_grad, axis=0, keepdims=True)
            score_grads[r, c] = (probs * (prob_grad - delta)).astype(jnp.bfloat16)
        return carry

    lax.fori_loop(0, pairs, soften, 0)

    def results(c, carry):
        upper = lax.broadcasted_iota(jnp.int32, (width, HEAD), 0) < span_len
        both = pl.ds(pl.multiple_of(c * width, width), width)
        for r in range(chain):
            rows, key, value, query, grad = fetch(r, c)
            low, score_grad = lows[r, c], score_grads[r, c]
            for h in range(2):
                mine = upper if h == 0 else jnp.logical_not(upper)
                key_part = jnp.dot(
                    score_grad,
                    jnp.where(mine, query, jnp.zeros_like(query)),
                    preferred_element_type=jnp.float32,
                )
                value_part = jnp.dot(
                    low,
                    jnp.where(mine, grad, jnp.zeros_like(grad)),
                    preferred_element_type=jnp.float32,
                )
                for n in range(2):
                    part = slice(n * length, (n + 1) * length)
                    grads[rows[h][n], :, :HEAD] += key_part[part]
                    grads[rows[h][n], :, HEAD:] += value_part[part]
            attended = jnp.where(upper, dot_0(low, value[0]), dot_0(low, value[1]))
            query_grad = jnp.where(upper, dot_0(score_grad, key[0]), dot_0(score_grad, key[1]))
            given[r][0, both, :] = attended.astype(jnp.bfloat16)
            given[r][1, both, :] = (query_grad * inverse_root).astype(jnp.bfloat16)
        return carry

    lax.fori_loop(0, pairs, results, 0)
    again[:, pl.ds(0, tokens), :] = given[chain - 1][...]
    again[:, pl.ds(tokens, TILE), :] = jnp.zeros((2, TILE, HEAD), jnp.bfloat16)
    for member in range(chain):
        for s in range(slots):
            part = pl.ds(s * length, length)
            own = member * 2 * slots + y * slots + s
            other = member * 2 * slots + (1 - y) * slots + s
            kept[member, part, :HEAD] = grads[own, :, :HEAD] * inverse_root
            kept[member, part, HEAD:] = grads[own, :, HEAD:]
            sent[member, part, :HEAD] = (grads[other, :, :HEAD] * inverse_root).astype(jnp.bfloat16)
            sent[member, part, HEAD:] = grads[other, :, HEAD:].astype(jnp.bfloat16)


def turn_kernel(*refs):
    count = len(refs) // 2
    for share, result in zip(refs[:count], refs[count:]):
        half = result.shape[1]
        for side in range(2):
            result[side] = share[:, side * half:(side + 1) * half].T


def inner(place):
    return (place[0] == 1) | (place[0] == 2)


def weigh_kernel(chain, wants, place, *refs):
    shares, refs = refs[:chain], refs[chain + 1:]
    sources, targets = refs[:-len(wants)], refs[-len(wants):]

    def multiply(row_grad):
        for want, target in zip(wants, targets):
            half = place[1] if want else 1 - place[1]
            total = sum(
                jnp.dot(
                    shares[q][half],
                    row_grad[place[0] ^ mask(place[2] ^ q)],
                    preferred_element_type=jnp.float32,
                )
                for q in range(chain)
            )
            target[...] = total.astype(target.dtype)

    if len(sources) == 1:
        multiply(sources[0])
    else:
        pl.when(inner(place))(lambda: multiply(sources[0]))
        pl.when(jnp.logical_not(inner(place)))(lambda: multiply(sources[1]))


def collect_kernel(chain, place, *refs):
    count = chain - 1
    kept, received, (key_grad, value_grad) = refs[:count], refs[count:2 * count], refs[2 * count:]
    a = place[0]
    turned = inner(place).astype(jnp.int32)
    for r, head in enumerate((a, a ^ 1, a ^ (2 + turned))):
        total = kept[r][...] + received[r][...].astype(jnp.float32)
        key_grad[:, column(head)] = total[:, :HEAD]
        value_grad[:, column(head)] = total[:, HEAD:]


def finish_kernel(chain, place, kept, received, near, far, *refs):
    targets, (total, sems) = refs[4:8], refs[8:]
    apart = inner(place)

    def write(part):
        copies = [
            pltpu.make_async_copy(
                part.at[side, pl.ds(0, targets[side].shape[0]), :],
                targets[side].at[:, column(place[0] ^ (chain - 1))],
                sems.at[side],
            )
            for side in range(2)
        ]
        for copy in copies:
            copy.start()
        total[...] = kept[...] + received[...].astype(jnp.float32)
        copies += [
            pltpu.make_async_copy(
                total.at[:, pl.ds(side * HEAD, HEAD)],
                targets[2 + side].at[:, column(place[0] ^ (3 - apart.astype(jnp.int32)))],
                sems.at[2 + side],
            )
            for side in range(2)
        ]
        for copy in copies[2:]:
            copy.start()
        for copy in copies:
            copy.wait()

    pl.when(apart)(lambda: write(near))
    pl.when(jnp.logical_not(apart))(lambda: write(far))


def sum_kernel(kept, received, *refs):
    total = refs[-1]
    total[...] = (kept[...] + received[...].astype(jnp.float32)).astype(jnp.bfloat16)


def estimate(us):
    return pl.CostEstimate(
        flops=int(us * 1e9), bytes_accessed=int(us * 3.5e6), transcendentals=0
    )


def gate(arrays, tokens):
    n = len(arrays)
    return pl.pallas_call(
        lambda *refs: None,
        out_shape=[jax.ShapeDtypeStruct(x.shape, x.dtype) for x in arrays],
        in_specs=[ANY] * (n + len(tokens)),
        out_specs=[ANY] * n,
        input_output_aliases={i: i for i in range(n)},
        compiler_params=params(1),
        cost_estimate=estimate(0.5),
        name="gate",
    )(*arrays, *tokens)


def chained(queries, out_grad, owner, store_row, store, norm_gain, w_key, w_value):
    stored, length, width = store.shape
    spans, neighbours_per = owner.shape
    peers, groups = lax.axis_size("dp"), lax.axis_size("mp")
    chain = peers // 2
    tokens = queries.shape[0]
    rows = stored * length
    features = w_key.shape[0]
    position, m = lax.axis_index("dp"), lax.axis_index("mp")
    place = jnp.stack([position // 2, position % 2, m]).astype(jnp.int32)

    def held(x):
        return pltpu.with_memory_space_constraint(x, pltpu.HBM)

    def along(x, r):
        return lax.ppermute(x, "dp", [(i, i ^ (2 * r)) for i in range(peers)])

    def hop(x, pairs):
        return lax.ppermute(
            x, "dp", [(2 * i + y, 2 * j + y) for i, j in pairs for y in range(2)]
        )

    def across(x):
        return lax.ppermute(x, "dp", [(i, i ^ 1) for i in range(peers)])

    def beside(x, q):
        return lax.ppermute(x, "mp", [(i, i ^ q) for i in range(groups)])

    *packed, mine = pl.pallas_call(
        functools.partial(pack_kernel, chain, stored),
        out_shape=[
            jax.ShapeDtypeStruct((2 * tokens + spans * neighbours_per, HEAD), queries.dtype)
        ] * chain
        + [jax.ShapeDtypeStruct((rows + TILE, width), store.dtype)],
        in_specs=[SMEM] * 3 + [HBM] * 3 + [VMEM],
        out_specs=[VMEM] * (chain + 1),
        scratch_shapes=[pltpu.SemaphoreType.DMA((chain, 2)), pltpu.SemaphoreType.DMA],
        compiler_params=params(8),
        cost_estimate=estimate(1),
        name="pack",
    )(
        place,
        held(owner.T),
        held(store_row.T),
        held(queries),
        held(out_grad),
        held(store.reshape(rows, width)),
        held(norm_gain),
    )
    arrived = [beside(mine, q) for q in range(2, groups, 2)]
    swapped = beside(mine, 1)
    asked = [packed[0]] + [along(packed[r], r) for r in range(1, chain - 1)]
    *arrived, late = gate(arrived + [packed[chain - 1]], asked[1:])
    asked.append(along(late, chain - 1))
    states = [mine, swapped]
    for x in arrived:
        states += [x, beside(x, 1)]

    *encoded, normed_own = pl.pallas_call(
        functools.partial(project_kernel, chain, features),
        out_shape=[jax.ShapeDtypeStruct((rows, 2 * HEAD), jnp.bfloat16)] * chain
        + [jax.ShapeDtypeStruct((rows, width), jnp.bfloat16)],
        in_specs=[SMEM, HBM, HBM] + [VMEM] * groups,
        out_specs=[VMEM] * (chain + 1),
        scratch_shapes=[
            pltpu.VMEM((rows, features), jnp.bfloat16),
            pltpu.VMEM((chain, features, 2 * HEAD), jnp.bfloat16),
            pltpu.SemaphoreType.DMA((chain, 2)),
        ],
        compiler_params=params(24),
        cost_estimate=estimate(6),
        name="project",
    )(place, held(w_key), held(w_value), *states)

    near = [encoded[0]] + [along(encoded[r], r) for r in range(1, chain)]
    far = [across(x) for x in near]

    (normed_own,) = gate([normed_own], near)
    turned = lax.ppermute(
        normed_own,
        ("dp", "mp"),
        [
            (i * groups + j, (i ^ (2 * MASKS[j])) * groups + j)
            for i in range(peers)
            for j in range(groups)
        ],
    )

    side_by_side = (chain, spans // 2, neighbours_per * length, 2 * tokens // spans)
    *given, again, kept, sent = pl.pallas_call(
        functools.partial(attend_kernel, chain, spans, stored, length),
        out_shape=[jax.ShapeDtypeStruct((2, tokens, HEAD), queries.dtype)] * chain
        + [jax.ShapeDtypeStruct((2, tokens + TILE, HEAD), queries.dtype)]
        + [
            jax.ShapeDtypeStruct((chain, rows, 2 * HEAD), jnp.float32),
            jax.ShapeDtypeStruct((chain, rows, 2 * HEAD), jnp.bfloat16),
        ],
        in_specs=[SMEM] + [VMEM] * (3 * chain),
        out_specs=[VMEM] * (chain + 3),
        scratch_shapes=[
            pltpu.VMEM((peers * stored, length, 2 * HEAD), jnp.bfloat16),
            pltpu.VMEM((peers * stored, length, 2 * HEAD), jnp.float32),
            pltpu.VMEM(side_by_side, jnp.float32),
            pltpu.VMEM(side_by_side, jnp.float32),
            pltpu.VMEM(side_by_side, jnp.bfloat16),
            pltpu.VMEM(side_by_side, jnp.bfloat16),
            pltpu.VMEM((chain, spans * neighbours_per, HEAD), jnp.int32),
            pltpu.SMEM((chain, spans * neighbours_per, HEAD), jnp.int32),
            pltpu.SemaphoreType.DMA,
        ],
        compiler_params=params(28),
        cost_estimate=estimate(14),
        name="attend",
    )(place, *asked, *near, *far)

    received = across(sent)
    returned = [given[0]] + [along(given[r], r) for r in range(1, chain - 1)]
    row_grad = pl.pallas_call(
        sum_kernel,
        out_shape=jax.ShapeDtypeStruct((chain, rows, 2 * HEAD), jnp.bfloat16),
        in_specs=[VMEM, VMEM, ANY, ANY, ANY],
        out_specs=VMEM,
        compiler_params=params(8),
        cost_estimate=estimate(1),
        name="sum",
    )(kept, received, returned[1], returned[2], turned)
    middle, outward, ahead = ((1, 2), (2, 1)), ((2, 3), (1, 0)), ((0, 1), (3, 2))
    beyond, inward = along(row_grad, 1), hop(row_grad, middle)
    onward = hop(beyond, middle)
    row_grads = [
        [row_grad],
        [beyond],
        [inward, hop(inward, outward)],
        [onward, hop(onward, outward)],
    ]

    shares = [turned, beside(turned, 1)]
    for q in range(2, groups, 2):
        x = beside(turned, q)
        shares += [x, beside(x, 1)]
    shares = pl.pallas_call(
        turn_kernel,
        out_shape=[jax.ShapeDtypeStruct((2, width // 2, rows), jnp.bfloat16)] * groups,
        in_specs=[VMEM] * groups,
        out_specs=[VMEM] * groups,
        compiler_params=params(8),
        cost_estimate=estimate(0.1),
        name="turn",
    )(*shares)

    def weigh(sources, wants, token):
        types = [jnp.float32 if want else jnp.bfloat16 for want in wants]
        return pl.pallas_call(
            functools.partial(weigh_kernel, chain, wants),
            out_shape=[jax.ShapeDtypeStruct((width // 2, 2 * HEAD), t) for t in types],
            in_specs=[SMEM] + [VMEM] * groups + [ANY] + [VMEM] * len(sources),
            out_specs=[VMEM] * len(wants),
            compiler_params=params(12),
            cost_estimate=estimate(len(wants)),
            name="weigh",
        )(place, *shares, token, *sources)

    (again,) = gate([again], [beyond])
    passing = hop(again, ahead)

    kept, received, token = [], [], place
    for sources in row_grads[:-1]:
        own, other = weigh(sources, (True, False), token)
        kept.append(own)
        received.append(across(other))
        token = received[-2] if len(received) > 1 else own
        if len(kept) == 2:
            (passing,) = gate([passing], [onward])
            passing = hop(passing, middle)
    passing, late = gate([passing, given[-1]], [received[1]])
    (other,) = weigh(row_grads[-1], (False,), passing)
    far, near = hop(passing, outward), hop(late, middle)
    received.append(across(other))
    (own,) = weigh(row_grads[-1], (True,), other)
    kept.append(own)
    answers = [jax.ShapeDtypeStruct(queries.shape, queries.dtype)] * 2
    attended, query_grad = pl.pallas_call(
        functools.partial(unpack_kernel, chain),
        out_shape=answers,
        in_specs=[SMEM] + [VMEM] * (chain - 1),
        out_specs=[VMEM] * 2,
        compiler_params=params(8),
        cost_estimate=estimate(2),
        name="unpack",
    )(place, *returned[:chain - 1])
    results = [jax.ShapeDtypeStruct((width // 2, chain * HEAD), jnp.float32)] * 2
    key_grad, value_grad = pl.pallas_call(
        functools.partial(collect_kernel, chain),
        out_shape=results,
        in_specs=[SMEM] + [VMEM] * (2 * chain - 2),
        out_specs=[VMEM] * 2,
        compiler_params=params(12),
        cost_estimate=estimate(2),
        name="collect",
    )(place, *kept[:-1], *received[:-1])
    return pl.pallas_call(
        functools.partial(finish_kernel, chain),
        out_shape=answers + results,
        in_specs=[SMEM] + [VMEM] * 4 + [ANY] * 4,
        out_specs=[ANY] * 4,
        scratch_shapes=[
            pltpu.VMEM((width // 2, 2 * HEAD), jnp.float32),
            pltpu.SemaphoreType.DMA((4,)),
        ],
        input_output_aliases={5 + i: i for i in range(4)},
        compiler_params=params(4),
        cost_estimate=estimate(1),
        name="finish",
    )(
        place,
        kept[-1],
        received[-1],
        near,
        far,
        attended,
        query_grad,
        key_grad,
        value_grad,
    )


def gathered(queries, out_grad, owner, store_row, store, norm_gain, w_key, w_value):
    whole_store, whole_gain = (
        lax.all_gather(store, "mp", axis=2, tiled=True),
        lax.all_gather(norm_gain, "mp", axis=0, tiled=True),
    )
    stored, length, model_width = whole_store.shape
    floats = whole_store.astype(jnp.float32)
    scale_rows = lax.rsqrt(jnp.mean(floats * floats, axis=-1, keepdims=True) + epsilon)
    normed = (
        (floats * scale_rows * whole_gain.astype(jnp.float32))
        .astype(jnp.bfloat16)
        .reshape(stored * length, model_width)
    )
    columns_half = w_key.shape[1]
    key_rows = jnp.dot(normed, w_key, preferred_element_type=jnp.float32).astype(jnp.bfloat16)
    value_rows = jnp.dot(normed, w_value, preferred_element_type=jnp.float32).astype(jnp.bfloat16)
    encoded = jnp.concatenate([key_rows, value_rows], axis=1).reshape(
        stored, length, 2 * columns_half
    )
    spans, neighbours_per = owner.shape
    references = spans * neighbours_per
    peer_count = lax.axis_size("dp")
    own_flat = owner.reshape(references)
    row_flat = store_row.reshape(references)
    global_id = own_flat * stored + row_flat
    earlier = jnp.tril(jnp.ones((references, references), jnp.int32), -1)
    everything = lax.all_gather(encoded, "dp", axis=0, tiled=True)
    context = jnp.take(everything, global_id, axis=0)
    head_size = HEAD
    heads_here = columns_half // head_size
    context_all = context.reshape(spans, neighbours_per * length, 2, heads_here, head_size)
    key_ctx = context_all[:, :, 0]
    value_ctx = context_all[:, :, 1]
    tokens = queries.reshape(spans, -1, heads_here, head_size)
    grads_out = out_grad.reshape(spans, -1, heads_here, head_size)
    inverse_root = 1.0 / math.sqrt(head_size)
    scores = (
        jnp.einsum("cqhd,ckhd->chqk", tokens, key_ctx, preferred_element_type=jnp.float32)
        * inverse_root
    )
    probs = jax.nn.softmax(scores, axis=-1)
    probs_low = probs.astype(jnp.bfloat16)
    attended = (
        jnp.einsum("chqk,ckhd->cqhd", probs_low, value_ctx, preferred_element_type=jnp.float32)
        .astype(jnp.bfloat16)
        .reshape(queries.shape)
    )
    prob_grad = jnp.einsum(
        "cqhd,ckhd->chqk", grads_out, value_ctx, preferred_element_type=jnp.float32
    )
    row_delta = jnp.sum(probs * prob_grad, axis=-1, keepdims=True)
    score_grad = (probs * (prob_grad - row_delta)).astype(jnp.bfloat16)
    query_grad = (
        (
            jnp.einsum("chqk,ckhd->cqhd", score_grad, key_ctx, preferred_element_type=jnp.float32)
            * inverse_root
        )
        .astype(jnp.bfloat16)
        .reshape(queries.shape)
    )
    key_grad = (
        jnp.einsum("chqk,cqhd->ckhd", score_grad, tokens, preferred_element_type=jnp.float32)
        * inverse_root
    )
    value_grad = jnp.einsum(
        "chqk,cqhd->ckhd", probs_low, grads_out, preferred_element_type=jnp.float32
    )
    ref_grads = jnp.stack([key_grad, value_grad], axis=2).reshape(
        references, length, 2 * columns_half
    )
    same_id = (global_id[:, None] == global_id[None, :]).astype(jnp.float32)
    first_use = jnp.sum(same_id * earlier.astype(jnp.float32), axis=1) == 0.0
    summed = jnp.einsum("ij,jtc->itc", same_id, ref_grads, precision=lax.Precision.HIGHEST)
    sent_grads = jnp.where(first_use[:, None, None], summed, 0.0).astype(jnp.bfloat16)
    placement_table = (global_id[:, None] == jnp.arange(peer_count * stored)[None, :]).astype(
        jnp.bfloat16
    )
    dense_grads = jnp.einsum(
        "ir,itc->rtc", placement_table, sent_grads, preferred_element_type=jnp.float32
    )
    row_grad = lax.psum_scatter(
        dense_grads.astype(jnp.bfloat16), "dp", scatter_dimension=0, tiled=True
    )
    row_grad_low = row_grad.reshape(stored * length, 2 * columns_half)
    weight_grad = lax.psum_scatter(
        lax.dot_general(
            normed, row_grad_low, (((0,), (0,)), ((), ())), preferred_element_type=jnp.float32
        ).astype(jnp.bfloat16),
        "dp",
        scatter_dimension=0,
        tiled=True,
    ).astype(jnp.float32)
    return (attended, query_grad, weight_grad[:, :columns_half], weight_grad[:, columns_half:])


def solution(mesh):
    in_specs = (
        P("dp", "mp"),
        P("dp", "mp"),
        P("dp", None),
        P("dp", None),
        P("dp", None, "mp"),
        P("mp"),
        P(None, "mp"),
        P(None, "mp"),
    )
    out_specs = (P("dp", "mp"), P("dp", "mp"), P("dp", "mp"), P("dp", "mp"))
    def shards(*args):
        peers, groups = lax.axis_size("dp"), lax.axis_size("mp")
        heads_here = args[6].shape[1] // HEAD
        if peers == 2 * heads_here == 2 * groups == 8:
            return chained(*args)
        return gathered(*args)

    return jax.shard_map(shards, mesh=mesh, in_specs=in_specs, out_specs=out_specs, check_vma=False)
```

```python
import functools
import math

import jax
import jax.numpy as jnp
from jax import lax
from jax.experimental import pallas as pl
from jax.experimental.pallas import tpu as pltpu
from jax.sharding import PartitionSpec as P

HEAD = 128
TILE = 16


epsilon = 1e-06

def params(mebibytes):
    return pltpu.CompilerParams(vmem_limit_bytes=mebibytes * 1024 * 1024)


VMEM = pl.BlockSpec(memory_space=pltpu.VMEM)
SMEM = pl.BlockSpec(memory_space=pltpu.SMEM)
ANY = pl.BlockSpec(memory_space=pl.ANY)
HBM = pl.BlockSpec(memory_space=pltpu.HBM)


def column(head):
    return pl.ds(pl.multiple_of(head * HEAD, HEAD), HEAD)


def pack_kernel(chain, slots, place, owner, store_row, queries, out_grad, store, gain, *refs):
    packed, (bundle, sems, sem) = refs[:chain], refs[chain:]
    tokens, rows = queries.shape[0], store.shape[0]
    named, spans = owner.shape
    copies = [pltpu.make_async_copy(store, bundle.at[pl.ds(0, rows), :], sem)] + [
        pltpu.make_async_copy(
            source.at[:, column(place[0] ^ r)],
            packed[r].at[pl.ds(side * tokens, tokens), :],
            sems.at[r, side],
        )
        for r in range(chain)
        for side, source in enumerate((queries, out_grad))
    ]
    for copy in copies:
        copy.start()
    bundle[pl.ds(rows, TILE), :] = jnp.broadcast_to(gain[...].reshape(1, store.shape[1]), (TILE, store.shape[1]))
    line = lax.broadcasted_iota(jnp.int32, (spans * named, HEAD), 0)
    block = jnp.zeros((spans * named, HEAD), jnp.int32)
    for i in range(spans * named):
        spot = (i % named, i // named)
        block = jnp.where(line == i, owner[spot] * slots + store_row[spot], block)
    block = block.astype(jnp.float32).astype(jnp.bfloat16)
    for r in range(chain):
        packed[r][pl.ds(2 * tokens, spans * named), :] = block
    for copy in copies:
        copy.wait()


def unpack_kernel(chain, place, *refs):
    parts, (attended, query_grad) = refs[:chain - 1], refs[chain - 1:]
    for r, part in enumerate(parts):
        attended[:, column(place[0] ^ r)] = part[0]
        query_grad[:, column(place[0] ^ r)] = part[1]


MASKS = (0, 3, 1, 2)


def mask(m):
    return sum(jnp.where(m == i, x, 0) for i, x in enumerate(MASKS))


def project_kernel(chain, features, place, w_key, w_value, *refs):
    shards = len(refs) - chain - 4
    states, refs = refs[:shards], refs[shards:]
    encoded, (normed_own, normed, weights, sems) = refs[:chain], refs[chain:]
    copies = [
        pltpu.make_async_copy(
            source.at[:, column(place[0] ^ r)],
            weights.at[r, :, pl.ds(side * HEAD, HEAD)],
            sems.at[r, side],
        )
        for r in range(chain)
        for side, source in enumerate((w_key, w_value))
    ]
    for copy in copies:
        copy.start()
    m = place[2]
    rows, width = normed_own.shape
    gain = [x[pl.ds(rows, TILE), :].astype(jnp.float32) for x in states]

    def norm_tile(i, carry):
        part = pl.ds(pl.multiple_of(i * TILE, TILE), TILE)
        square = jnp.zeros((TILE, 1), jnp.float32)
        for x in states:
            floats = x[part, :].astype(jnp.float32)
            square += jnp.sum(floats * floats, axis=-1, keepdims=True)
        scale = lax.rsqrt(square / features + epsilon)
        for q, x in enumerate(states):
            low = (x[part, :].astype(jnp.float32) * scale * gain[q]).astype(jnp.bfloat16)
            normed[part, pl.ds(pl.multiple_of((m ^ q) * width, width), width)] = low
        return carry

    lax.fori_loop(0, rows // TILE, norm_tile, 0, unroll=2)
    block = place[0] ^ mask(m)
    normed_own[...] = normed[:, pl.ds(pl.multiple_of(block * width, width), width)]
    for r in range(chain):
        copies[2 * r].wait()
        copies[2 * r + 1].wait()
        encoded[r][...] = jnp.dot(
            normed[...], weights[r], preferred_element_type=jnp.float32
        ).astype(jnp.bfloat16)


def dot_t(left, right):
    return lax.dot_general(
        left, right, (((1,), (1,)), ((), ())), preferred_element_type=jnp.float32
    )


def dot_0(left, right):
    return lax.dot_general(
        left, right, (((0,), (0,)), ((), ())), preferred_element_type=jnp.float32
    )


def attend_kernel(chain, spans, slots, length, place, *refs):
    asked, refs = refs[:chain], refs[chain:]
    near, far, refs = refs[:chain], refs[chain:2 * chain], refs[2 * chain:]
    given, again, refs = refs[:chain], refs[chain], refs[chain + 1:]
    kept, sent, context, grads, scores, prob_grads, lows, score_grads, lines, ids, sem = refs
    a, y = place[0], place[1]
    tokens = given[0].shape[1]
    span_len = tokens // spans
    pairs = spans // 2
    width = 2 * span_len
    named = 2 * spans
    inverse_root = 1.0 / math.sqrt(HEAD)
    for r in range(chain):
        lines[r] = asked[r][pl.ds(2 * tokens, named), :].astype(jnp.float32).astype(jnp.int32)
    copy = pltpu.make_async_copy(lines, ids, sem)
    copy.start()
    for r in range(chain):
        first = (a ^ r) * 2 * slots
        for s in range(slots):
            context[first + y * slots + s] = near[r][pl.ds(s * length, length), :]
            context[first + (1 - y) * slots + s] = far[r][pl.ds(s * length, length), :]
    grads[...] = jnp.zeros_like(grads)
    copy.wait()

    def fetch(r, c):
        rows = [[ids[r, 4 * c + 2 * h + n, 0] for n in range(2)] for h in range(2)]
        key = [jnp.concatenate([context[i, :, :HEAD] for i in row], axis=0) for row in rows]
        value = [jnp.concatenate([context[i, :, HEAD:] for i in row], axis=0) for row in rows]
        query = asked[r][pl.ds(pl.multiple_of(c * width, width), width), :]
        grad = asked[r][pl.ds(pl.multiple_of(tokens + c * width, width), width), :]
        return rows, key, value, query, grad

    def products(c, carry):
        first = lax.broadcasted_iota(jnp.int32, (2 * length, width), 1) < span_len
        for r in range(chain):
            rows, key, value, query, grad = fetch(r, c)
            scores[r, c] = jnp.where(first, dot_t(key[0], query), dot_t(key[1], query))
            prob_grads[r, c] = jnp.where(first, dot_t(value[0], grad), dot_t(value[1], grad))
        return carry

    lax.fori_loop(0, pairs, products, 0)

    def soften(c, carry):
        for r in range(chain):
            score = scores[r, c] * inverse_root
            powers = jnp.exp(score - jnp.max(score, axis=0, keepdims=True))
            probs = powers * (1.0 / jnp.sum(powers, axis=0, keepdims=True))
            lows[r, c] = probs.astype(jnp.bfloat16)
            prob_grad = prob_grads[r, c]
            delta = jnp.sum(probs * prob_grad, axis=0, keepdims=True)
            score_grads[r, c] = (probs * (prob_grad - delta)).astype(jnp.bfloat16)
        return carry

    lax.fori_loop(0, pairs, soften, 0)

    def results(c, carry):
        upper = lax.broadcasted_iota(jnp.int32, (width, HEAD), 0) < span_len
        both = pl.ds(pl.multiple_of(c * width, width), width)
        for r in range(chain):
            rows, key, value, query, grad = fetch(r, c)
            low, score_grad = lows[r, c], score_grads[r, c]
            for h in range(2):
                mine = upper if h == 0 else jnp.logical_not(upper)
                key_part = jnp.dot(
                    score_grad,
                    jnp.where(mine, query, jnp.zeros_like(query)),
                    preferred_element_type=jnp.float32,
                )
                value_part = jnp.dot(
                    low,
                    jnp.where(mine, grad, jnp.zeros_like(grad)),
                    preferred_element_type=jnp.float32,
                )
                for n in range(2):
                    part = slice(n * length, (n + 1) * length)
                    grads[rows[h][n], :, :HEAD] += key_part[part]
                    grads[rows[h][n], :, HEAD:] += value_part[part]
            attended = jnp.where(upper, dot_0(low, value[0]), dot_0(low, value[1]))
            query_grad = jnp.where(upper, dot_0(score_grad, key[0]), dot_0(score_grad, key[1]))
            given[r][0, both, :] = attended.astype(jnp.bfloat16)
            given[r][1, both, :] = (query_grad * inverse_root).astype(jnp.bfloat16)
        return carry

    lax.fori_loop(0, pairs, results, 0)
    again[:, pl.ds(0, tokens), :] = given[chain - 1][...]
    again[:, pl.ds(tokens, TILE), :] = jnp.zeros((2, TILE, HEAD), jnp.bfloat16)
    for member in range(chain):
        for s in range(slots):
            part = pl.ds(s * length, length)
            own = member * 2 * slots + y * slots + s
            other = member * 2 * slots + (1 - y) * slots + s
            kept[member, part, :HEAD] = grads[own, :, :HEAD] * inverse_root
            kept[member, part, HEAD:] = grads[own, :, HEAD:]
            sent[member, part, :HEAD] = (grads[other, :, :HEAD] * inverse_root).astype(jnp.bfloat16)
            sent[member, part, HEAD:] = grads[other, :, HEAD:].astype(jnp.bfloat16)


def turn_kernel(*refs):
    count = len(refs) // 2
    for share, result in zip(refs[:count], refs[count:]):
        half = result.shape[1]
        for side in range(2):
            result[side] = share[:, side * half:(side + 1) * half].T


def inner(place):
    return (place[0] == 1) | (place[0] == 2)


def weigh_kernel(chain, wants, place, *refs):
    shares, refs = refs[:chain], refs[chain + 1:]
    sources, targets = refs[:-len(wants)], refs[-len(wants):]

    def multiply(row_grad):
        for want, target in zip(wants, targets):
            half = place[1] if want else 1 - place[1]
            total = sum(
                jnp.dot(
                    shares[q][half],
                    row_grad[place[0] ^ mask(place[2] ^ q)],
                    preferred_element_type=jnp.float32,
                )
                for q in range(chain)
            )
            target[...] = total.astype(target.dtype)

    if len(sources) == 1:
        multiply(sources[0])
    else:
        pl.when(inner(place))(lambda: multiply(sources[0]))
        pl.when(jnp.logical_not(inner(place)))(lambda: multiply(sources[1]))


def collect_kernel(chain, place, *refs):
    count = chain - 1
    kept, received, (key_grad, value_grad) = refs[:count], refs[count:2 * count], refs[2 * count:]
    a = place[0]
    turned = inner(place).astype(jnp.int32)
    for r, head in enumerate((a, a ^ 1, a ^ (2 + turned))):
        total = kept[r][...] + received[r][...].astype(jnp.float32)
        key_grad[:, column(head)] = total[:, :HEAD]
        value_grad[:, column(head)] = total[:, HEAD:]


def finish_kernel(chain, place, kept, received, near, far, *refs):
    targets, (total, sems) = refs[4:8], refs[8:]
    apart = inner(place)

    def write(part):
        copies = [
            pltpu.make_async_copy(
                part.at[side, pl.ds(0, targets[side].shape[0]), :],
                targets[side].at[:, column(place[0] ^ (chain - 1))],
                sems.at[side],
            )
            for side in range(2)
        ]
        for copy in copies:
            copy.start()
        total[...] = kept[...] + received[...].astype(jnp.float32)
        copies += [
            pltpu.make_async_copy(
                total.at[:, pl.ds(side * HEAD, HEAD)],
                targets[2 + side].at[:, column(place[0] ^ (3 - apart.astype(jnp.int32)))],
                sems.at[2 + side],
            )
            for side in range(2)
        ]
        for copy in copies[2:]:
            copy.start()
        for copy in copies:
            copy.wait()

    pl.when(apart)(lambda: write(near))
    pl.when(jnp.logical_not(apart))(lambda: write(far))


def sum_kernel(kept, received, *refs):
    total = refs[-1]
    total[...] = (kept[...] + received[...].astype(jnp.float32)).astype(jnp.bfloat16)


def estimate(us):
    return pl.CostEstimate(
        flops=int(us * 1e9), bytes_accessed=int(us * 3.5e6), transcendentals=0
    )


def gate(arrays, tokens):
    n = len(arrays)
    return pl.pallas_call(
        lambda *refs: None,
        out_shape=[jax.ShapeDtypeStruct(x.shape, x.dtype) for x in arrays],
        in_specs=[ANY] * (n + len(tokens)),
        out_specs=[ANY] * n,
        input_output_aliases={i: i for i in range(n)},
        compiler_params=params(1),
        cost_estimate=estimate(0.5),
        name="gate",
    )(*arrays, *tokens)


def chained(queries, out_grad, owner, store_row, store, norm_gain, w_key, w_value):
    stored, length, width = store.shape
    spans, neighbours_per = owner.shape
    peers, groups = lax.axis_size("dp"), lax.axis_size("mp")
    chain = peers // 2
    tokens = queries.shape[0]
    rows = stored * length
    features = w_key.shape[0]
    position, m = lax.axis_index("dp"), lax.axis_index("mp")
    place = jnp.stack([position // 2, position % 2, m]).astype(jnp.int32)

    def held(x):
        return pltpu.with_memory_space_constraint(x, pltpu.HBM)

    def along(x, r):
        return lax.ppermute(x, "dp", [(i, i ^ (2 * r)) for i in range(peers)])

    def hop(x, pairs):
        return lax.ppermute(
            x, "dp", [(2 * i + y, 2 * j + y) for i, j in pairs for y in range(2)]
        )

    def across(x):
        return lax.ppermute(x, "dp", [(i, i ^ 1) for i in range(peers)])

    def beside(x, q):
        return lax.ppermute(x, "mp", [(i, i ^ q) for i in range(groups)])

    *packed, mine = pl.pallas_call(
        functools.partial(pack_kernel, chain, stored),
        out_shape=[
            jax.ShapeDtypeStruct((2 * tokens + spans * neighbours_per, HEAD), queries.dtype)
        ] * chain
        + [jax.ShapeDtypeStruct((rows + TILE, width), store.dtype)],
        in_specs=[SMEM] * 3 + [HBM] * 3 + [VMEM],
        out_specs=[VMEM] * (chain + 1),
        scratch_shapes=[pltpu.SemaphoreType.DMA((chain, 2)), pltpu.SemaphoreType.DMA],
        compiler_params=params(8),
        cost_estimate=estimate(1),
        name="pack",
    )(
        place,
        held(owner.T),
        held(store_row.T),
        held(queries),
        held(out_grad),
        held(store.reshape(rows, width)),
        held(norm_gain),
    )
    arrived = [beside(mine, q) for q in range(2, groups, 2)]
    swapped = beside(mine, 1)
    asked = [packed[0]] + [along(packed[r], r) for r in range(1, chain - 1)]
    *arrived, late = gate(arrived + [packed[chain - 1]], asked[1:])
    asked.append(along(late, chain - 1))
    states = [mine, swapped]
    for x in arrived:
        states += [x, beside(x, 1)]

    *encoded, normed_own = pl.pallas_call(
        functools.partial(project_kernel, chain, features),
        out_shape=[jax.ShapeDtypeStruct((rows, 2 * HEAD), jnp.bfloat16)] * chain
        + [jax.ShapeDtypeStruct((rows, width), jnp.bfloat16)],
        in_specs=[SMEM, HBM, HBM] + [VMEM] * groups,
        out_specs=[VMEM] * (chain + 1),
        scratch_shapes=[
            pltpu.VMEM((rows, features), jnp.bfloat16),
            pltpu.VMEM((chain, features, 2 * HEAD), jnp.bfloat16),
            pltpu.SemaphoreType.DMA((chain, 2)),
        ],
        compiler_params=params(24),
        cost_estimate=estimate(6),
        name="project",
    )(place, held(w_key), held(w_value), *states)

    near = [encoded[0]] + [along(encoded[r], r) for r in range(1, chain)]
    far = [across(x) for x in near]

    (normed_own,) = gate([normed_own], near)
    turned = lax.ppermute(
        normed_own,
        ("dp", "mp"),
        [
            (i * groups + j, (i ^ (2 * MASKS[j])) * groups + j)
            for i in range(peers)
            for j in range(groups)
        ],
    )

    side_by_side = (chain, spans // 2, neighbours_per * length, 2 * tokens // spans)
    *given, again, kept, sent = pl.pallas_call(
        functools.partial(attend_kernel, chain, spans, stored, length),
        out_shape=[jax.ShapeDtypeStruct((2, tokens, HEAD), queries.dtype)] * chain
        + [jax.ShapeDtypeStruct((2, tokens + TILE, HEAD), queries.dtype)]
        + [
            jax.ShapeDtypeStruct((chain, rows, 2 * HEAD), jnp.float32),
            jax.ShapeDtypeStruct((chain, rows, 2 * HEAD), jnp.bfloat16),
        ],
        in_specs=[SMEM] + [VMEM] * (3 * chain),
        out_specs=[VMEM] * (chain + 3),
        scratch_shapes=[
            pltpu.VMEM((peers * stored, length, 2 * HEAD), jnp.bfloat16),
            pltpu.VMEM((peers * stored, length, 2 * HEAD), jnp.float32),
            pltpu.VMEM(side_by_side, jnp.float32),
            pltpu.VMEM(side_by_side, jnp.float32),
            pltpu.VMEM(side_by_side, jnp.bfloat16),
            pltpu.VMEM(side_by_side, jnp.bfloat16),
            pltpu.VMEM((chain, spans * neighbours_per, HEAD), jnp.int32),
            pltpu.SMEM((chain, spans * neighbours_per, HEAD), jnp.int32),
            pltpu.SemaphoreType.DMA,
        ],
        compiler_params=params(28),
        cost_estimate=estimate(14),
        name="attend",
    )(place, *asked, *near, *far)

    received = across(sent)
    returned = [given[0]] + [along(given[r], r) for r in range(1, chain - 1)]
    row_grad = pl.pallas_call(
        sum_kernel,
        out_shape=jax.ShapeDtypeStruct((chain, rows, 2 * HEAD), jnp.bfloat16),
        in_specs=[VMEM, VMEM, ANY, ANY, ANY],
        out_specs=VMEM,
        compiler_params=params(8),
        cost_estimate=estimate(1),
        name="sum",
    )(kept, received, returned[1], returned[2], turned)
    middle, outward, ahead = ((1, 2), (2, 1)), ((2, 3), (1, 0)), ((0, 1), (3, 2))
    beyond, inward = along(row_grad, 1), hop(row_grad, middle)
    onward = hop(beyond, middle)
    row_grads = [
        [row_grad],
        [beyond],
        [inward, hop(inward, outward)],
        [onward, hop(onward, outward)],
    ]

    shares = [turned, beside(turned, 1)]
    for q in range(2, groups, 2):
        x = beside(turned, q)
        shares += [x, beside(x, 1)]
    shares = pl.pallas_call(
        turn_kernel,
        out_shape=[jax.ShapeDtypeStruct((2, width // 2, rows), jnp.bfloat16)] * groups,
        in_specs=[VMEM] * groups,
        out_specs=[VMEM] * groups,
        compiler_params=params(8),
        cost_estimate=estimate(0.1),
        name="turn",
    )(*shares)

    def weigh(sources, wants, token):
        types = [jnp.float32 if want else jnp.bfloat16 for want in wants]
        return pl.pallas_call(
            functools.partial(weigh_kernel, chain, wants),
            out_shape=[jax.ShapeDtypeStruct((width // 2, 2 * HEAD), t) for t in types],
            in_specs=[SMEM] + [VMEM] * groups + [ANY] + [VMEM] * len(sources),
            out_specs=[VMEM] * len(wants),
            compiler_params=params(12),
            cost_estimate=estimate(len(wants)),
            name="weigh",
        )(place, *shares, token, *sources)

    (again,) = gate([again], [beyond])
    passing = hop(again, ahead)

    kept, received, token = [], [], place
    for sources in row_grads[:-1]:
        own, other = weigh(sources, (True, False), token)
        kept.append(own)
        received.append(across(other))
        token = received[-2] if len(received) > 1 else own
        if len(kept) == 2:
            late, passing = gate([given[-1], passing], [onward, own])
            returned.append(hop(late, middle))
            passing = hop(passing, middle)
    (passing,) = gate([passing], [kept[2]])
    (other,) = weigh(row_grads[-1], (False,), passing)
    far = hop(passing, outward)
    received.append(across(other))
    (own,) = weigh(row_grads[-1], (True,), other)
    kept.append(own)
    answers = [jax.ShapeDtypeStruct(queries.shape, queries.dtype)] * 2
    attended, query_grad = pl.pallas_call(
        functools.partial(unpack_kernel, chain),
        out_shape=answers,
        in_specs=[SMEM] + [VMEM] * (chain - 1),
        out_specs=[VMEM] * 2,
        compiler_params=params(8),
        cost_estimate=estimate(2),
        name="unpack",
    )(place, *returned[:chain - 1])
    results = [jax.ShapeDtypeStruct((width // 2, chain * HEAD), jnp.float32)] * 2
    key_grad, value_grad = pl.pallas_call(
        functools.partial(collect_kernel, chain),
        out_shape=results,
        in_specs=[SMEM] + [VMEM] * (2 * chain - 2),
        out_specs=[VMEM] * 2,
        compiler_params=params(12),
        cost_estimate=estimate(2),
        name="collect",
    )(place, *kept[:-1], *received[:-1])
    return pl.pallas_call(
        functools.partial(finish_kernel, chain),
        out_shape=answers + results,
        in_specs=[SMEM] + [VMEM] * 4 + [ANY] * 4,
        out_specs=[ANY] * 4,
        scratch_shapes=[
            pltpu.VMEM((width // 2, 2 * HEAD), jnp.float32),
            pltpu.SemaphoreType.DMA((4,)),
        ],
        input_output_aliases={5 + i: i for i in range(4)},
        compiler_params=params(4),
        cost_estimate=estimate(1),
        name="finish",
    )(
        place,
        kept[-1],
        received[-1],
        returned[-1],
        far,
        attended,
        query_grad,
        key_grad,
        value_grad,
    )


def gathered(queries, out_grad, owner, store_row, store, norm_gain, w_key, w_value):
    whole_store, whole_gain = (
        lax.all_gather(store, "mp", axis=2, tiled=True),
        lax.all_gather(norm_gain, "mp", axis=0, tiled=True),
    )
    stored, length, model_width = whole_store.shape
    floats = whole_store.astype(jnp.float32)
    scale_rows = lax.rsqrt(jnp.mean(floats * floats, axis=-1, keepdims=True) + epsilon)
    normed = (
        (floats * scale_rows * whole_gain.astype(jnp.float32))
        .astype(jnp.bfloat16)
        .reshape(stored * length, model_width)
    )
    columns_half = w_key.shape[1]
    key_rows = jnp.dot(normed, w_key, preferred_element_type=jnp.float32).astype(jnp.bfloat16)
    value_rows = jnp.dot(normed, w_value, preferred_element_type=jnp.float32).astype(jnp.bfloat16)
    encoded = jnp.concatenate([key_rows, value_rows], axis=1).reshape(
        stored, length, 2 * columns_half
    )
    spans, neighbours_per = owner.shape
    references = spans * neighbours_per
    peer_count = lax.axis_size("dp")
    own_flat = owner.reshape(references)
    row_flat = store_row.reshape(references)
    global_id = own_flat * stored + row_flat
    earlier = jnp.tril(jnp.ones((references, references), jnp.int32), -1)
    everything = lax.all_gather(encoded, "dp", axis=0, tiled=True)
    context = jnp.take(everything, global_id, axis=0)
    head_size = HEAD
    heads_here = columns_half // head_size
    context_all = context.reshape(spans, neighbours_per * length, 2, heads_here, head_size)
    key_ctx = context_all[:, :, 0]
    value_ctx = context_all[:, :, 1]
    tokens = queries.reshape(spans, -1, heads_here, head_size)
    grads_out = out_grad.reshape(spans, -1, heads_here, head_size)
    inverse_root = 1.0 / math.sqrt(head_size)
    scores = (
        jnp.einsum("cqhd,ckhd->chqk", tokens, key_ctx, preferred_element_type=jnp.float32)
        * inverse_root
    )
    probs = jax.nn.softmax(scores, axis=-1)
    probs_low = probs.astype(jnp.bfloat16)
    attended = (
        jnp.einsum("chqk,ckhd->cqhd", probs_low, value_ctx, preferred_element_type=jnp.float32)
        .astype(jnp.bfloat16)
        .reshape(queries.shape)
    )
    prob_grad = jnp.einsum(
        "cqhd,ckhd->chqk", grads_out, value_ctx, preferred_element_type=jnp.float32
    )
    row_delta = jnp.sum(probs * prob_grad, axis=-1, keepdims=True)
    score_grad = (probs * (prob_grad - row_delta)).astype(jnp.bfloat16)
    query_grad = (
        (
            jnp.einsum("chqk,ckhd->cqhd", score_grad, key_ctx, preferred_element_type=jnp.float32)
            * inverse_root
        )
        .astype(jnp.bfloat16)
        .reshape(queries.shape)
    )
    key_grad = (
        jnp.einsum("chqk,cqhd->ckhd", score_grad, tokens, preferred_element_type=jnp.float32)
        * inverse_root
    )
    value_grad = jnp.einsum(
        "chqk,cqhd->ckhd", probs_low, grads_out, preferred_element_type=jnp.float32
    )
    ref_grads = jnp.stack([key_grad, value_grad], axis=2).reshape(
        references, length, 2 * columns_half
    )
    same_id = (global_id[:, None] == global_id[None, :]).astype(jnp.float32)
    first_use = jnp.sum(same_id * earlier.astype(jnp.float32), axis=1) == 0.0
    summed = jnp.einsum("ij,jtc->itc", same_id, ref_grads, precision=lax.Precision.HIGHEST)
    sent_grads = jnp.where(first_use[:, None, None], summed, 0.0).astype(jnp.bfloat16)
    placement_table = (global_id[:, None] == jnp.arange(peer_count * stored)[None, :]).astype(
        jnp.bfloat16
    )
    dense_grads = jnp.einsum(
        "ir,itc->rtc", placement_table, sent_grads, preferred_element_type=jnp.float32
    )
    row_grad = lax.psum_scatter(
        dense_grads.astype(jnp.bfloat16), "dp", scatter_dimension=0, tiled=True
    )
    row_grad_low = row_grad.reshape(stored * length, 2 * columns_half)
    weight_grad = lax.psum_scatter(
        lax.dot_general(
            normed, row_grad_low, (((0,), (0,)), ((), ())), preferred_element_type=jnp.float32
        ).astype(jnp.bfloat16),
        "dp",
        scatter_dimension=0,
        tiled=True,
    ).astype(jnp.float32)
    return (attended, query_grad, weight_grad[:, :columns_half], weight_grad[:, columns_half:])


def solution(mesh):
    in_specs = (
        P("dp", "mp"),
        P("dp", "mp"),
        P("dp", None),
        P("dp", None),
        P("dp", None, "mp"),
        P("mp"),
        P(None, "mp"),
        P(None, "mp"),
    )
    out_specs = (P("dp", "mp"), P("dp", "mp"), P("dp", "mp"), P("dp", "mp"))
    def shards(*args):
        peers, groups = lax.axis_size("dp"), lax.axis_size("mp")
        heads_here = args[6].shape[1] // HEAD
        if peers == 2 * heads_here == 2 * groups == 8:
            return chained(*args)
        return gathered(*args)

    return jax.shard_map(shards, mesh=mesh, in_specs=in_specs, out_specs=out_specs, check_vma=False)
```

```python
import functools
import math

import jax
import jax.numpy as jnp
from jax import lax
from jax.experimental import pallas as pl
from jax.experimental.pallas import tpu as pltpu
from jax.sharding import PartitionSpec as P

HEAD = 128
TILE = 16


epsilon = 1e-06

def params(mebibytes):
    return pltpu.CompilerParams(vmem_limit_bytes=mebibytes * 1024 * 1024)


VMEM = pl.BlockSpec(memory_space=pltpu.VMEM)
SMEM = pl.BlockSpec(memory_space=pltpu.SMEM)
ANY = pl.BlockSpec(memory_space=pl.ANY)
HBM = pl.BlockSpec(memory_space=pltpu.HBM)


def column(head):
    return pl.ds(pl.multiple_of(head * HEAD, HEAD), HEAD)


def pack_kernel(chain, slots, owner, store_row, queries, out_grad, store, gain, *refs):
    packed, (bundle, sems, sem) = refs[:chain], refs[chain:]
    tokens, rows = queries.shape[0], store.shape[0]
    named, spans = owner.shape
    member = lax.axis_index("dp") // 2
    copies = [pltpu.make_async_copy(store, bundle.at[pl.ds(0, rows), :], sem)] + [
        pltpu.make_async_copy(
            source.at[:, column(member ^ r)],
            packed[r].at[pl.ds(side * tokens, tokens), :],
            sems.at[r, side],
        )
        for r in range(chain)
        for side, source in enumerate((queries, out_grad))
    ]
    for copy in copies:
        copy.start()
    bundle[pl.ds(rows, TILE), :] = jnp.broadcast_to(gain[...].reshape(1, store.shape[1]), (TILE, store.shape[1]))
    line = lax.broadcasted_iota(jnp.int32, (spans * named, HEAD), 0)
    block = jnp.zeros((spans * named, HEAD), jnp.int32)
    for i in range(spans * named):
        spot = (i % named, i // named)
        block = jnp.where(line == i, owner[spot] * slots + store_row[spot], block)
    block = block.astype(jnp.float32).astype(jnp.bfloat16)
    for r in range(chain):
        packed[r][pl.ds(2 * tokens, spans * named), :] = block
    for copy in copies:
        copy.wait()


def unpack_kernel(chain, place, *refs):
    parts, (attended, query_grad) = refs[:chain - 1], refs[chain - 1:]
    for r, part in enumerate(parts):
        attended[:, column(place[0] ^ r)] = part[0]
        query_grad[:, column(place[0] ^ r)] = part[1]


MASKS = (0, 3, 1, 2)


def mask(m):
    return sum(jnp.where(m == i, x, 0) for i, x in enumerate(MASKS))


def project_kernel(chain, features, place, w_key, w_value, *refs):
    shards = len(refs) - chain - 4
    states, refs = refs[:shards], refs[shards:]
    encoded, (normed_own, normed, weights, sems) = refs[:chain], refs[chain:]
    copies = [
        pltpu.make_async_copy(
            source.at[:, column(place[0] ^ r)],
            weights.at[r, :, pl.ds(side * HEAD, HEAD)],
            sems.at[r, side],
        )
        for r in range(chain)
        for side, source in enumerate((w_key, w_value))
    ]
    for copy in copies:
        copy.start()
    m = place[2]
    rows, width = normed_own.shape
    gain = [x[pl.ds(rows, TILE), :].astype(jnp.float32) for x in states]

    def norm_tile(i, carry):
        part = pl.ds(pl.multiple_of(i * TILE, TILE), TILE)
        square = jnp.zeros((TILE, 1), jnp.float32)
        for x in states:
            floats = x[part, :].astype(jnp.float32)
            square += jnp.sum(floats * floats, axis=-1, keepdims=True)
        scale = lax.rsqrt(square / features + epsilon)
        for q, x in enumerate(states):
            low = (x[part, :].astype(jnp.float32) * scale * gain[q]).astype(jnp.bfloat16)
            normed[part, pl.ds(pl.multiple_of((m ^ q) * width, width), width)] = low
        return carry

    lax.fori_loop(0, rows // TILE, norm_tile, 0, unroll=2)
    block = place[0] ^ mask(m)
    normed_own[...] = normed[:, pl.ds(pl.multiple_of(block * width, width), width)]
    for r in range(chain):
        copies[2 * r].wait()
        copies[2 * r + 1].wait()
        encoded[r][...] = jnp.dot(
            normed[...], weights[r], preferred_element_type=jnp.float32
        ).astype(jnp.bfloat16)


def dot_t(left, right):
    return lax.dot_general(
        left, right, (((1,), (1,)), ((), ())), preferred_element_type=jnp.float32
    )


def dot_0(left, right):
    return lax.dot_general(
        left, right, (((0,), (0,)), ((), ())), preferred_element_type=jnp.float32
    )


def attend_kernel(chain, spans, slots, length, place, *refs):
    asked, refs = refs[:chain], refs[chain:]
    near, far, refs = refs[:chain], refs[chain:2 * chain], refs[2 * chain:]
    given, again, refs = refs[:chain], refs[chain], refs[chain + 1:]
    kept, sent, context, grads, scores, prob_grads, lows, score_grads, lines, ids, sem = refs
    a, y = place[0], place[1]
    tokens = given[0].shape[1]
    span_len = tokens // spans
    pairs = spans // 2
    width = 2 * span_len
    named = 2 * spans
    inverse_root = 1.0 / math.sqrt(HEAD)
    for r in range(chain):
        lines[r] = asked[r][pl.ds(2 * tokens, named), :].astype(jnp.float32).astype(jnp.int32)
    copy = pltpu.make_async_copy(lines, ids, sem)
    copy.start()
    for r in range(chain):
        first = (a ^ r) * 2 * slots
        for s in range(slots):
            context[first + y * slots + s] = near[r][pl.ds(s * length, length), :]
            context[first + (1 - y) * slots + s] = far[r][pl.ds(s * length, length), :]
    grads[...] = jnp.zeros_like(grads)
    copy.wait()

    def fetch(r, c):
        rows = [[ids[r, 4 * c + 2 * h + n, 0] for n in range(2)] for h in range(2)]
        key = [jnp.concatenate([context[i, :, :HEAD] for i in row], axis=0) for row in rows]
        value = [jnp.concatenate([context[i, :, HEAD:] for i in row], axis=0) for row in rows]
        query = asked[r][pl.ds(pl.multiple_of(c * width, width), width), :]
        grad = asked[r][pl.ds(pl.multiple_of(tokens + c * width, width), width), :]
        return rows, key, value, query, grad

    def products(c, carry):
        first = lax.broadcasted_iota(jnp.int32, (2 * length, width), 1) < span_len
        for r in range(chain):
            rows, key, value, query, grad = fetch(r, c)
            scores[r, c] = jnp.where(first, dot_t(key[0], query), dot_t(key[1], query))
            prob_grads[r, c] = jnp.where(first, dot_t(value[0], grad), dot_t(value[1], grad))
        return carry

    lax.fori_loop(0, pairs, products, 0)

    def soften(c, carry):
        for r in range(chain):
            score = scores[r, c] * inverse_root
            powers = jnp.exp(score - jnp.max(score, axis=0, keepdims=True))
            probs = powers * (1.0 / jnp.sum(powers, axis=0, keepdims=True))
            lows[r, c] = probs.astype(jnp.bfloat16)
            prob_grad = prob_grads[r, c]
            delta = jnp.sum(probs * prob_grad, axis=0, keepdims=True)
            score_grads[r, c] = (probs * (prob_grad - delta)).astype(jnp.bfloat16)
        return carry

    lax.fori_loop(0, pairs, soften, 0)

    def results(c, carry):
        upper = lax.broadcasted_iota(jnp.int32, (width, HEAD), 0) < span_len
        both = pl.ds(pl.multiple_of(c * width, width), width)
        for r in range(chain):
            rows, key, value, query, grad = fetch(r, c)
            low, score_grad = lows[r, c], score_grads[r, c]
            for h in range(2):
                mine = upper if h == 0 else jnp.logical_not(upper)
                key_part = jnp.dot(
                    score_grad,
                    jnp.where(mine, query, jnp.zeros_like(query)),
                    preferred_element_type=jnp.float32,
                )
                value_part = jnp.dot(
                    low,
                    jnp.where(mine, grad, jnp.zeros_like(grad)),
                    preferred_element_type=jnp.float32,
                )
                for n in range(2):
                    part = slice(n * length, (n + 1) * length)
                    grads[rows[h][n], :, :HEAD] += key_part[part]
                    grads[rows[h][n], :, HEAD:] += value_part[part]
            attended = jnp.where(upper, dot_0(low, value[0]), dot_0(low, value[1]))
            query_grad = jnp.where(upper, dot_0(score_grad, key[0]), dot_0(score_grad, key[1]))
            given[r][0, both, :] = attended.astype(jnp.bfloat16)
            given[r][1, both, :] = (query_grad * inverse_root).astype(jnp.bfloat16)
        return carry

    lax.fori_loop(0, pairs, results, 0)
    again[...] = given[chain - 1][...]
    for member in range(chain):
        for s in range(slots):
            part = pl.ds(s * length, length)
            own = member * 2 * slots + y * slots + s
            other = member * 2 * slots + (1 - y) * slots + s
            kept[member, part, :HEAD] = grads[own, :, :HEAD] * inverse_root
            kept[member, part, HEAD:] = grads[own, :, HEAD:]
            sent[member, part, :HEAD] = (grads[other, :, :HEAD] * inverse_root).astype(jnp.bfloat16)
            sent[member, part, HEAD:] = grads[other, :, HEAD:].astype(jnp.bfloat16)


def turn_kernel(*refs):
    count = len(refs) // 2
    for share, result in zip(refs[:count], refs[count:]):
        half = result.shape[1]
        for side in range(2):
            result[side] = share[:, side * half:(side + 1) * half].T


def inner(place):
    return (place[0] == 1) | (place[0] == 2)


def weigh_kernel(chain, wants, place, *refs):
    shares, refs = refs[:chain], refs[chain + 1:]
    sources, targets = refs[:-len(wants)], refs[-len(wants):]

    def multiply(row_grad):
        for want, target in zip(wants, targets):
            half = place[1] if want else 1 - place[1]
            total = sum(
                jnp.dot(
                    shares[q][half],
                    row_grad[place[0] ^ mask(place[2] ^ q)],
                    preferred_element_type=jnp.float32,
                )
                for q in range(chain)
            )
            target[...] = total.astype(target.dtype)

    if len(sources) == 1:
        multiply(sources[0])
    else:
        pl.when(inner(place))(lambda: multiply(sources[0]))
        pl.when(jnp.logical_not(inner(place)))(lambda: multiply(sources[1]))


def collect_kernel(chain, place, *refs):
    count = chain - 1
    kept, received, (key_grad, value_grad) = refs[:count], refs[count:2 * count], refs[2 * count:]
    a = place[0]
    turned = inner(place).astype(jnp.int32)
    for r, head in enumerate((a, a ^ 1, a ^ (2 + turned))):
        total = kept[r][...] + received[r][...].astype(jnp.float32)
        key_grad[:, column(head)] = total[:, :HEAD]
        value_grad[:, column(head)] = total[:, HEAD:]


def finish_kernel(chain, place, kept, received, near, far, *refs):
    targets, (total, sems) = refs[4:8], refs[8:]
    apart = inner(place)

    def write(part):
        copies = [
            pltpu.make_async_copy(
                part.at[side], targets[side].at[:, column(place[0] ^ (chain - 1))], sems.at[side]
            )
            for side in range(2)
        ]
        for copy in copies:
            copy.start()
        total[...] = kept[...] + received[...].astype(jnp.float32)
        copies += [
            pltpu.make_async_copy(
                total.at[:, pl.ds(side * HEAD, HEAD)],
                targets[2 + side].at[:, column(place[0] ^ (3 - apart.astype(jnp.int32)))],
                sems.at[2 + side],
            )
            for side in range(2)
        ]
        for copy in copies[2:]:
            copy.start()
        for copy in copies:
            copy.wait()

    pl.when(apart)(lambda: write(near))
    pl.when(jnp.logical_not(apart))(lambda: write(far))


def sum_kernel(kept, received, *refs):
    total = refs[-1]
    total[...] = (kept[...] + received[...].astype(jnp.float32)).astype(jnp.bfloat16)


def estimate(us):
    return pl.CostEstimate(
        flops=int(us * 1e9), bytes_accessed=int(us * 3.5e6), transcendentals=0
    )


def gate(arrays, tokens):
    n = len(arrays)
    return pl.pallas_call(
        lambda *refs: None,
        out_shape=[jax.ShapeDtypeStruct(x.shape, x.dtype) for x in arrays],
        in_specs=[ANY] * (n + len(tokens)),
        out_specs=[ANY] * n,
        input_output_aliases={i: i for i in range(n)},
        compiler_params=params(1),
        cost_estimate=estimate(0.5),
        name="gate",
    )(*arrays, *tokens)


def chained(queries, out_grad, owner, store_row, store, norm_gain, w_key, w_value):
    stored, length, width = store.shape
    spans, neighbours_per = owner.shape
    peers, groups = lax.axis_size("dp"), lax.axis_size("mp")
    chain = peers // 2
    tokens = queries.shape[0]
    rows = stored * length
    features = w_key.shape[0]
    position, m = lax.axis_index("dp"), lax.axis_index("mp")
    place = jnp.stack([position // 2, position % 2, m]).astype(jnp.int32)

    def held(x):
        return pltpu.with_memory_space_constraint(x, pltpu.HBM)

    def along(x, r):
        return lax.ppermute(x, "dp", [(i, i ^ (2 * r)) for i in range(peers)])

    def hop(x, pairs):
        return lax.ppermute(
            x, "dp", [(2 * i + y, 2 * j + y) for i, j in pairs for y in range(2)]
        )

    def across(x):
        return lax.ppermute(x, "dp", [(i, i ^ 1) for i in range(peers)])

    def beside(x, q):
        return lax.ppermute(x, "mp", [(i, i ^ q) for i in range(groups)])

    *packed, mine = pl.pallas_call(
        functools.partial(pack_kernel, chain, stored),
        out_shape=[
            jax.ShapeDtypeStruct((2 * tokens + spans * neighbours_per, HEAD), queries.dtype)
        ] * chain
        + [jax.ShapeDtypeStruct((rows + TILE, width), store.dtype)],
        in_specs=[SMEM] * 2 + [HBM] * 3 + [VMEM],
        out_specs=[VMEM] * (chain + 1),
        scratch_shapes=[pltpu.SemaphoreType.DMA((chain, 2)), pltpu.SemaphoreType.DMA],
        compiler_params=params(8),
        cost_estimate=estimate(1),
        name="pack",
    )(
        held(owner.T),
        held(store_row.T),
        held(queries),
        held(out_grad),
        held(store.reshape(rows, width)),
        held(norm_gain),
    )
    arrived = [beside(mine, q) for q in range(2, groups, 2)]
    swapped = beside(mine, 1)
    asked = [packed[0]] + [along(packed[r], r) for r in range(1, chain - 1)]
    *arrived, late = gate(arrived + [packed[chain - 1]], asked[1:])
    asked.append(along(late, chain - 1))
    states = [mine, swapped]
    for x in arrived:
        states += [x, beside(x, 1)]

    *encoded, normed_own = pl.pallas_call(
        functools.partial(project_kernel, chain, features),
        out_shape=[jax.ShapeDtypeStruct((rows, 2 * HEAD), jnp.bfloat16)] * chain
        + [jax.ShapeDtypeStruct((rows, width), jnp.bfloat16)],
        in_specs=[SMEM, HBM, HBM] + [VMEM] * groups,
        out_specs=[VMEM] * (chain + 1),
        scratch_shapes=[
            pltpu.VMEM((rows, features), jnp.bfloat16),
            pltpu.VMEM((chain, features, 2 * HEAD), jnp.bfloat16),
            pltpu.SemaphoreType.DMA((chain, 2)),
        ],
        compiler_params=params(24),
        cost_estimate=estimate(6),
        name="project",
    )(place, held(w_key), held(w_value), *states)

    near = [encoded[0]] + [along(encoded[r], r) for r in range(1, chain)]
    far = [across(x) for x in near]

    (normed_own,) = gate([normed_own], near)
    turned = lax.ppermute(
        normed_own,
        ("dp", "mp"),
        [
            (i * groups + j, (i ^ (2 * MASKS[j])) * groups + j)
            for i in range(peers)
            for j in range(groups)
        ],
    )

    side_by_side = (chain, spans // 2, neighbours_per * length, 2 * tokens // spans)
    *given, again, kept, sent = pl.pallas_call(
        functools.partial(attend_kernel, chain, spans, stored, length),
        out_shape=[jax.ShapeDtypeStruct((2, tokens, HEAD), queries.dtype)] * (chain + 1)
        + [
            jax.ShapeDtypeStruct((chain, rows, 2 * HEAD), jnp.float32),
            jax.ShapeDtypeStruct((chain, rows, 2 * HEAD), jnp.bfloat16),
        ],
        in_specs=[SMEM] + [VMEM] * (3 * chain),
        out_specs=[VMEM] * (chain + 3),
        scratch_shapes=[
            pltpu.VMEM((peers * stored, length, 2 * HEAD), jnp.bfloat16),
            pltpu.VMEM((peers * stored, length, 2 * HEAD), jnp.float32),
            pltpu.VMEM(side_by_side, jnp.float32),
            pltpu.VMEM(side_by_side, jnp.float32),
            pltpu.VMEM(side_by_side, jnp.bfloat16),
            pltpu.VMEM(side_by_side, jnp.bfloat16),
            pltpu.VMEM((chain, spans * neighbours_per, HEAD), jnp.int32),
            pltpu.SMEM((chain, spans * neighbours_per, HEAD), jnp.int32),
            pltpu.SemaphoreType.DMA,
        ],
        compiler_params=params(28),
        cost_estimate=estimate(14),
        name="attend",
    )(place, *asked, *near, *far)

    received = across(sent)
    returned = [given[0]] + [along(given[r], r) for r in range(1, chain - 1)]
    row_grad = pl.pallas_call(
        sum_kernel,
        out_shape=jax.ShapeDtypeStruct((chain, rows, 2 * HEAD), jnp.bfloat16),
        in_specs=[VMEM, VMEM, ANY, ANY, ANY],
        out_specs=VMEM,
        compiler_params=params(8),
        cost_estimate=estimate(1),
        name="sum",
    )(kept, received, returned[1], returned[2], turned)
    middle, outward, ahead = ((1, 2), (2, 1)), ((2, 3), (1, 0)), ((0, 1), (3, 2))
    beyond, inward = along(row_grad, 1), hop(row_grad, middle)
    onward = hop(beyond, middle)
    row_grads = [
        [row_grad],
        [beyond],
        [inward, hop(inward, outward)],
        [onward, hop(onward, outward)],
    ]

    shares = [turned, beside(turned, 1)]
    for q in range(2, groups, 2):
        x = beside(turned, q)
        shares += [x, beside(x, 1)]
    shares = pl.pallas_call(
        turn_kernel,
        out_shape=[jax.ShapeDtypeStruct((2, width // 2, rows), jnp.bfloat16)] * groups,
        in_specs=[VMEM] * groups,
        out_specs=[VMEM] * groups,
        compiler_params=params(8),
        cost_estimate=estimate(0.1),
        name="turn",
    )(*shares)

    def weigh(sources, wants, token):
        types = [jnp.float32 if want else jnp.bfloat16 for want in wants]
        return pl.pallas_call(
            functools.partial(weigh_kernel, chain, wants),
            out_shape=[jax.ShapeDtypeStruct((width // 2, 2 * HEAD), t) for t in types],
            in_specs=[SMEM] + [VMEM] * groups + [ANY] + [VMEM] * len(sources),
            out_specs=[VMEM] * len(wants),
            compiler_params=params(12),
            cost_estimate=estimate(len(wants)),
            name="weigh",
        )(place, *shares, token, *sources)

    (again,) = gate([again], [beyond])
    passing = hop(again, ahead)

    kept, received, token = [], [], place
    for sources in row_grads[:-1]:
        own, other = weigh(sources, (True, False), token)
        kept.append(own)
        received.append(across(other))
        token = received[-2] if len(received) > 1 else own
        if len(kept) == 2:
            late, passing = gate([given[-1], passing], [onward, own])
            returned.append(hop(late, middle))
            passing = hop(passing, middle)
    (other,) = weigh(row_grads[-1], (False,), token)
    received.append(across(other))
    (own,) = weigh(row_grads[-1], (True,), other)
    kept.append(own)
    (passing,) = gate([passing], [other])
    returned.append(hop(passing, outward))
    answers = [jax.ShapeDtypeStruct(queries.shape, queries.dtype)] * 2
    attended, query_grad = pl.pallas_call(
        functools.partial(unpack_kernel, chain),
        out_shape=answers,
        in_specs=[SMEM] + [VMEM] * (chain - 1),
        out_specs=[VMEM] * 2,
        compiler_params=params(8),
        cost_estimate=estimate(2),
        name="unpack",
    )(place, *returned[:chain - 1])
    results = [jax.ShapeDtypeStruct((width // 2, chain * HEAD), jnp.float32)] * 2
    key_grad, value_grad = pl.pallas_call(
        functools.partial(collect_kernel, chain),
        out_shape=results,
        in_specs=[SMEM] + [VMEM] * (2 * chain - 2),
        out_specs=[VMEM] * 2,
        compiler_params=params(12),
        cost_estimate=estimate(2),
        name="collect",
    )(place, *kept[:-1], *received[:-1])
    return pl.pallas_call(
        functools.partial(finish_kernel, chain),
        out_shape=answers + results,
        in_specs=[SMEM] + [VMEM] * 4 + [ANY] * 4,
        out_specs=[ANY] * 4,
        scratch_shapes=[
            pltpu.VMEM((width // 2, 2 * HEAD), jnp.float32),
            pltpu.SemaphoreType.DMA((4,)),
        ],
        input_output_aliases={5 + i: i for i in range(4)},
        compiler_params=params(4),
        cost_estimate=estimate(1),
        name="finish",
    )(
        place,
        kept[-1],
        received[-1],
        *returned[chain - 1:],
        attended,
        query_grad,
        key_grad,
        value_grad,
    )


def gathered(queries, out_grad, owner, store_row, store, norm_gain, w_key, w_value):
    whole_store, whole_gain = (
        lax.all_gather(store, "mp", axis=2, tiled=True),
        lax.all_gather(norm_gain, "mp", axis=0, tiled=True),
    )
    stored, length, model_width = whole_store.shape
    floats = whole_store.astype(jnp.float32)
    scale_rows = lax.rsqrt(jnp.mean(floats * floats, axis=-1, keepdims=True) + epsilon)
    normed = (
        (floats * scale_rows * whole_gain.astype(jnp.float32))
        .astype(jnp.bfloat16)
        .reshape(stored * length, model_width)
    )
    columns_half = w_key.shape[1]
    key_rows = jnp.dot(normed, w_key, preferred_element_type=jnp.float32).astype(jnp.bfloat16)
    value_rows = jnp.dot(normed, w_value, preferred_element_type=jnp.float32).astype(jnp.bfloat16)
    encoded = jnp.concatenate([key_rows, value_rows], axis=1).reshape(
        stored, length, 2 * columns_half
    )
    spans, neighbours_per = owner.shape
    references = spans * neighbours_per
    peer_count = lax.axis_size("dp")
    own_flat = owner.reshape(references)
    row_flat = store_row.reshape(references)
    global_id = own_flat * stored + row_flat
    earlier = jnp.tril(jnp.ones((references, references), jnp.int32), -1)
    everything = lax.all_gather(encoded, "dp", axis=0, tiled=True)
    context = jnp.take(everything, global_id, axis=0)
    head_size = HEAD
    heads_here = columns_half // head_size
    context_all = context.reshape(spans, neighbours_per * length, 2, heads_here, head_size)
    key_ctx = context_all[:, :, 0]
    value_ctx = context_all[:, :, 1]
    tokens = queries.reshape(spans, -1, heads_here, head_size)
    grads_out = out_grad.reshape(spans, -1, heads_here, head_size)
    inverse_root = 1.0 / math.sqrt(head_size)
    scores = (
        jnp.einsum("cqhd,ckhd->chqk", tokens, key_ctx, preferred_element_type=jnp.float32)
        * inverse_root
    )
    probs = jax.nn.softmax(scores, axis=-1)
    probs_low = probs.astype(jnp.bfloat16)
    attended = (
        jnp.einsum("chqk,ckhd->cqhd", probs_low, value_ctx, preferred_element_type=jnp.float32)
        .astype(jnp.bfloat16)
        .reshape(queries.shape)
    )
    prob_grad = jnp.einsum(
        "cqhd,ckhd->chqk", grads_out, value_ctx, preferred_element_type=jnp.float32
    )
    row_delta = jnp.sum(probs * prob_grad, axis=-1, keepdims=True)
    score_grad = (probs * (prob_grad - row_delta)).astype(jnp.bfloat16)
    query_grad = (
        (
            jnp.einsum("chqk,ckhd->cqhd", score_grad, key_ctx, preferred_element_type=jnp.float32)
            * inverse_root
        )
        .astype(jnp.bfloat16)
        .reshape(queries.shape)
    )
    key_grad = (
        jnp.einsum("chqk,cqhd->ckhd", score_grad, tokens, preferred_element_type=jnp.float32)
        * inverse_root
    )
    value_grad = jnp.einsum(
        "chqk,cqhd->ckhd", probs_low, grads_out, preferred_element_type=jnp.float32
    )
    ref_grads = jnp.stack([key_grad, value_grad], axis=2).reshape(
        references, length, 2 * columns_half
    )
    same_id = (global_id[:, None] == global_id[None, :]).astype(jnp.float32)
    first_use = jnp.sum(same_id * earlier.astype(jnp.float32), axis=1) == 0.0
    summed = jnp.einsum("ij,jtc->itc", same_id, ref_grads, precision=lax.Precision.HIGHEST)
    sent_grads = jnp.where(first_use[:, None, None], summed, 0.0).astype(jnp.bfloat16)
    placement_table = (global_id[:, None] == jnp.arange(peer_count * stored)[None, :]).astype(
        jnp.bfloat16
    )
    dense_grads = jnp.einsum(
        "ir,itc->rtc", placement_table, sent_grads, preferred_element_type=jnp.float32
    )
    row_grad = lax.psum_scatter(
        dense_grads.astype(jnp.bfloat16), "dp", scatter_dimension=0, tiled=True
    )
    row_grad_low = row_grad.reshape(stored * length, 2 * columns_half)
    weight_grad = lax.psum_scatter(
        lax.dot_general(
            normed, row_grad_low, (((0,), (0,)), ((), ())), preferred_element_type=jnp.float32
        ).astype(jnp.bfloat16),
        "dp",
        scatter_dimension=0,
        tiled=True,
    ).astype(jnp.float32)
    return (attended, query_grad, weight_grad[:, :columns_half], weight_grad[:, columns_half:])


def solution(mesh):
    in_specs = (
        P("dp", "mp"),
        P("dp", "mp"),
        P("dp", None),
        P("dp", None),
        P("dp", None, "mp"),
        P("mp"),
        P(None, "mp"),
        P(None, "mp"),
    )
    out_specs = (P("dp", "mp"), P("dp", "mp"), P("dp", "mp"), P("dp", "mp"))
    def shards(*args):
        peers, groups = lax.axis_size("dp"), lax.axis_size("mp")
        heads_here = args[6].shape[1] // HEAD
        if peers == 2 * heads_here == 2 * groups == 8:
            return chained(*args)
        return gathered(*args)

    return jax.shard_map(shards, mesh=mesh, in_specs=in_specs, out_specs=out_specs, check_vma=False)
```
